32 devices in a mesh: call: 2 (over x), tm: 16 (over z, y, core).
Axes of the slice: x: 2, y: 2, z: 4, core: 2. Of those that a mesh axis runs over, the one named last changes fastest.
Arguments:
- frames: bfloat16 [2, 2048, 1024], P('call', 'tm'), may hold values from -6 to 6
- lengths: int32 [2], replicated, may hold values from 512 to 2048, as said below
- ln_attn_gain: float32 [1024], replicated, may hold values from 0.5 to 1.5
- w_qkv: bfloat16 [1024, 3072], P('tm'), may hold values from -0.1875 to 0.1875
- w_out: bfloat16 [1024, 1024], P('tm'), may hold values from -1.5 to 1.5
- ln_conv_gain: float32 [1024], replicated, may hold values from 0.5 to 1.5
- w_pw1: bfloat16 [1024, 2048], P('tm'), may hold values from -0.1875 to 0.1875
- dw_kernel: float32 [9, 1024], replicated, may hold values from -2 to 2
- bn_gain: float32 [1024], replicated, may hold values from 0.5 to 1.5
- bn_bias: float32 [1024], replicated, may hold values from -3 to 3
Outputs:
- attended: bfloat16 [2, 2048, 1024], P('call', 'tm')
- conv_act: bfloat16 [2, 2048, 1024], P('call', 'tm')
The draws below stay inside these ranges and needn't reach their ends.
Inputs may be any that keep to these rules, and one draw needn't show every extreme that they name: `lengths`: valid frames of each call; at least one call of the batch fills all 2048 frames.
All inputs are finite; a program needn't handle non-finite values.
Results may differ from the reference program's by a relative error of at most 0.009.
Values may be sent and summed in bfloat16 or wider, within the bound.
A program may use at most 64 MiB of HBM per device.

```python
import jax
import jax.numpy as jnp
from jax import lax

D = 1024
HEADS = 16
HEAD_DIM = 64
SPAN = 128
LEFT = 1024
KERNEL = 9
FRAMES = 2048
BATCH = 2


def draw_lengths(key, part):
    drawn = jax.random.randint(jax.random.fold_in(key, 11), (BATCH,), FRAMES // 4, FRAMES + 1, dtype=jnp.int32)
    chosen = jax.random.randint(jax.random.fold_in(key, 12), (), 0, BATCH, dtype=jnp.int32)
    slots = jnp.arange(BATCH, dtype=jnp.int32)
    return jnp.where(slots == chosen, jnp.int32(FRAMES), drawn).astype(jnp.int32)


def levels(stream_key, dims, pieces, least, high):
    level, own = 1.0, jax.random.fold_in(stream_key, 6)
    for axis_at, parts in pieces:
        heights = jnp.exp(jax.random.uniform(jax.random.fold_in(own, axis_at), (parts,), jnp.float32, least / len(pieces), high / len(pieces)))
        level = level * jnp.repeat(heights, dims[axis_at] // parts).reshape([-1 if axis == axis_at else 1 for axis in range(len(dims))])
    return level


def scatter_about(stream_key, shape, scale, limit, split=(), kind=jnp.bfloat16):
    values = scale * jax.random.normal(stream_key, shape, jnp.float32)
    if split:
        values = values * levels(stream_key, shape, split, -0.22, 0.18)
    return jnp.clip(values, -limit, limit).astype(kind)


def setup_inputs(seed: int = 0) -> dict:
    splits = jax.random.split(jax.random.key(seed), 11)
    frames = scatter_about(splits[0], (BATCH, FRAMES, D), 1.0, 6.0, ((0, 2), (1, 16)))
    lengths = draw_lengths(jax.random.fold_in(splits[10], 71), 0)
    ln_attn_gain = jnp.clip(1.0 + 0.1 * jax.random.normal(splits[2], (D,), jnp.float32), 0.5, 1.5)
    w_qkv = scatter_about(splits[3], (D, 3 * D), D ** -0.5, 0.1875, ((0, 16),))
    w_out = scatter_about(splits[4], (D, D), (D // 64) ** -0.5, 1.5, ((0, 16),))
    ln_conv_gain = jnp.clip(1.0 + 0.1 * jax.random.normal(splits[5], (D,), jnp.float32), 0.5, 1.5)
    w_pw1 = scatter_about(splits[6], (D, 2 * D), D ** -0.5, 0.1875, ((0, 16),))
    dw_kernel = scatter_about(splits[7], (KERNEL, D), KERNEL ** -0.5, 2.0, (), jnp.float32)
    bn_gain = jnp.clip(1.0 + 0.1 * jax.random.normal(splits[8], (D,), jnp.float32), 0.5, 1.5)
    bn_bias = scatter_about(splits[9], (D,), 0.5, 3.0, (), jnp.float32)
    return {"frames": frames, "lengths": lengths, "ln_attn_gain": ln_attn_gain, "w_qkv": w_qkv, "w_out": w_out, "ln_conv_gain": ln_conv_gain, "w_pw1": w_pw1, "dw_kernel": dw_kernel, "bn_gain": bn_gain, "bn_bias": bn_bias}


def layer_norm(values, gain_vec):
    wide = values.astype(jnp.float32)
    center = wide - lax.optimization_barrier(jnp.mean(wide, axis=-1, keepdims=True))
    spread = lax.optimization_barrier(jnp.mean(center * center, axis=-1, keepdims=True))
    return center * lax.rsqrt(spread + 1e-05) * gain_vec

def reference(frames, lengths, ln_attn_gain, w_qkv, w_out, ln_conv_gain, w_pw1, dw_kernel, bn_gain, bn_bias):
    positions = jnp.arange(FRAMES, dtype=jnp.int32)
    half = KERNEL // 2

    def first_pass(operands):
        call_frames, length = operands
        frame_valid = positions < length
        normed = layer_norm(call_frames, ln_attn_gain).astype(jnp.bfloat16)
        packed = jnp.dot(normed, w_qkv, preferred_element_type=jnp.float32)
        queries = packed[:, :D].astype(jnp.bfloat16)
        keys_own = packed[:, D:2 * D].astype(jnp.bfloat16)
        values_own = packed[:, 2 * D:].astype(jnp.bfloat16)
        lead = jnp.zeros((LEFT, D), jnp.bfloat16)
        keys_pad = jnp.concatenate([lead, keys_own], axis=0)
        values_pad = jnp.concatenate([lead, values_own], axis=0)

        def block(block_index):
            block_first = (block_index * SPAN).astype(jnp.int32)
            query_block = lax.dynamic_slice_in_dim(queries, block_first, SPAN, 0)
            key_block = lax.dynamic_slice_in_dim(keys_pad, block_first, LEFT + SPAN, 0)
            value_block = lax.dynamic_slice_in_dim(values_pad, block_first, LEFT + SPAN, 0)
            key_pos = block_first - LEFT + jnp.arange(LEFT + SPAN, dtype=jnp.int32)
            query_pos = block_first + jnp.arange(SPAN, dtype=jnp.int32)
            allowed = (key_pos[None, :] >= 0) & ((key_pos[None, :] < length) | (key_pos[None, :] == query_pos[:, None]))
            query_heads = query_block.reshape(SPAN, HEADS, HEAD_DIM).astype(jnp.float32)
            key_heads = key_block.reshape(LEFT + SPAN, HEADS, HEAD_DIM).astype(jnp.float32)
            value_heads = value_block.reshape(LEFT + SPAN, HEADS, HEAD_DIM).astype(jnp.float32)
            scores = jnp.einsum('qhd,khd->hqk', query_heads, key_heads) / jnp.sqrt(jnp.float32(HEAD_DIM))
            raised = jnp.where(allowed[None], jnp.exp(scores), 0.0)
            probs = (raised / lax.optimization_barrier(jnp.sum(raised, axis=-1, keepdims=True))).astype(jnp.bfloat16)
            context = jnp.einsum('hqk,khd->qhd', probs.astype(jnp.float32), value_heads)
            return context.reshape(SPAN, D).astype(jnp.bfloat16)
        context = lax.map(block, jnp.arange(FRAMES // SPAN, dtype=jnp.int32)).reshape(FRAMES, D)
        projected = jnp.dot(context, w_out, preferred_element_type=jnp.float32)
        attended = jnp.where(frame_valid[:, None], call_frames.astype(jnp.float32) + projected, 0.0).astype(jnp.bfloat16)
        conv_in = layer_norm(attended, ln_conv_gain).astype(jnp.bfloat16)
        expanded = jnp.dot(conv_in, w_pw1, preferred_element_type=jnp.float32)
        gated = expanded[:, :D] * jax.nn.sigmoid(expanded[:, D:])
        gated = jnp.where(frame_valid[:, None], gated, 0.0).astype(jnp.bfloat16)
        return (attended, gated)
    attended, gated = lax.map(first_pass, (frames, lengths))

    def depthwise_of(gated_call):
        padded = jnp.pad(gated_call, ((half, half), (0, 0)))
        result = jnp.zeros((FRAMES, D), jnp.float32)
        for tap_index in range(KERNEL):
            result = result + padded[tap_index:tap_index + FRAMES].astype(jnp.float32) * dw_kernel[tap_index]
        return result

    def moments(operands):
        gated_call, length = operands
        depthwise = depthwise_of(gated_call)
        masked = jnp.where((positions < length)[:, None], depthwise, 0.0)
        return (lax.optimization_barrier(jnp.sum(masked, axis=0)), lax.optimization_barrier(jnp.sum(masked * depthwise, axis=0)))
    first_moment, second_moment = lax.map(moments, (gated, lengths))
    count_all = jnp.sum(lengths).astype(jnp.float32)
    average = lax.optimization_barrier(jnp.sum(first_moment, axis=0)) / count_all
    second = lax.optimization_barrier(jnp.sum(second_moment, axis=0)) / count_all

    def finish(operands):
        gated_call, length = operands
        depthwise = depthwise_of(gated_call)
        normal_act = (depthwise - average) * lax.rsqrt(second - average * average + 1e-05) * bn_gain + bn_bias
        activated = normal_act * jax.nn.sigmoid(normal_act)
        return jnp.where((positions < length)[:, None], activated, 0.0).astype(jnp.bfloat16)
    conv_act = lax.map(finish, (gated, lengths))
    return (attended, conv_act)
```

```python
import functools

import jax
import jax.numpy as jnp
from jax import lax
from jax.experimental import pallas as pl
from jax.experimental.pallas import tpu as pltpu
from jax.sharding import PartitionSpec as P

HEAD_DIM = 64
SPAN = 128
LEFT = 1024
KERNEL = 9


def passed_along(value, axis, steps):
    count = lax.axis_size(axis)
    first, last = (max(0, -steps), min(count, count - steps))
    return lax.ppermute(value, axis, [(source, source + steps) for source in range(first, last)])


def with_halo(cells, sides, width):
    for axis, dim in sides:
        count = lax.axis_size(axis)
        ends = count - 1
        head = lax.slice_in_dim(cells, 0, width, axis=dim)
        tail = lax.slice_in_dim(cells, cells.shape[dim] - width, cells.shape[dim], axis=dim)
        cells = jnp.concatenate(
            [
                lax.ppermute(tail, axis, [(i, (i + 1) % count) for i in range(ends)]),
                cells,
                lax.ppermute(head, axis, [((i + 1) % count, i) for i in range(ends)]),
            ],
            axis=dim,
        )
    return cells


def layer_norm(values, gain_vec):
    wide = values.astype(jnp.float32)
    center = wide - jnp.mean(wide, axis=-1, keepdims=True)
    spread = jnp.mean(center * center, axis=-1, keepdims=True)
    return center * lax.rsqrt(spread + 1e-05) * gain_vec


def contract_with(left, rows_piece):
    return jnp.dot(left, rows_piece, preferred_element_type=jnp.float32)


def on_device(
    frames, lengths, ln_attn_gain, w_qkv, w_out, ln_conv_gain, w_pw1, dw_kernel, bn_gain, bn_bias
):
    stream = frames[0]
    frame_count, model_width = stream.shape
    head_count = model_width // HEAD_DIM
    length = lax.dynamic_index_in_dim(lengths, lax.axis_index("call"), 0, keepdims=False)
    first_row = lax.axis_index("tm") * frame_count
    query_pos = first_row + jnp.arange(frame_count, dtype=jnp.int32)
    frame_valid = query_pos < length
    normed = layer_norm(stream, ln_attn_gain).astype(jnp.bfloat16)
    prior_blocks = LEFT // frame_count
    packed = contract_with(normed, lax.all_gather(w_qkv, "tm", axis=0, tiled=True))
    queries = packed[:, :model_width].astype(jnp.bfloat16)
    key_value = jnp.stack(
        [
            packed[:, model_width : 2 * model_width].astype(jnp.bfloat16),
            packed[:, 2 * model_width :].astype(jnp.bfloat16),
        ]
    )
    blocks = []
    current = key_value
    for hop_index in range(prior_blocks):
        current = passed_along(current, "tm", 1)
        blocks.append(current)
    context_kv = jnp.concatenate(blocks[::-1] + [key_value], axis=1)
    key_count = context_kv.shape[1]
    key_pos = first_row - prior_blocks * frame_count + jnp.arange(key_count, dtype=jnp.int32)
    span_first = query_pos // SPAN * SPAN
    allowed = (key_pos[None, :] >= 0) & (key_pos[None, :] >= span_first[:, None] - LEFT)
    allowed = allowed & (key_pos[None, :] < span_first[:, None] + SPAN)
    allowed = allowed & ((key_pos[None, :] < length) | (key_pos[None, :] == query_pos[:, None]))
    group_size = 4
    group_count = head_count // group_size
    query_groups = queries.reshape(frame_count, group_count, group_size, HEAD_DIM).transpose(
        1, 0, 2, 3
    )
    key_groups = (
        context_kv[0].reshape(key_count, group_count, group_size, HEAD_DIM).transpose(1, 0, 2, 3)
    )
    value_groups = (
        context_kv[1].reshape(key_count, group_count, group_size, HEAD_DIM).transpose(1, 0, 2, 3)
    )
    scale_factor = 1.0 / jnp.sqrt(jnp.float32(HEAD_DIM))

    def attend_group(operands):
        query_part, key_part, value_part = operands
        scores = (
            jnp.einsum("qhd,khd->hqk", query_part, key_part, preferred_element_type=jnp.float32)
            * scale_factor
        )
        raised = jnp.where(allowed[None], jnp.exp(scores), 0.0)
        probs = (raised / jnp.sum(raised, axis=-1, keepdims=True)).astype(jnp.bfloat16)
        mixed = jnp.einsum("hqk,khd->qhd", probs, value_part, preferred_element_type=jnp.float32)
        return mixed.astype(jnp.bfloat16)

    context = lax.map(attend_group, (query_groups, key_groups, value_groups))
    context = context.transpose(1, 0, 2, 3).reshape(frame_count, model_width)
    projected = contract_with(context, lax.all_gather(w_out, "tm", axis=0, tiled=True))
    attended = jnp.where(frame_valid[:, None], stream.astype(jnp.float32) + projected, 0.0).astype(
        jnp.bfloat16
    )
    conv_in = layer_norm(attended, ln_conv_gain).astype(jnp.bfloat16)
    expanded = contract_with(conv_in, lax.all_gather(w_pw1, "tm", axis=0, tiled=True))
    gated = expanded[:, :model_width] * jax.nn.sigmoid(expanded[:, model_width:])
    gated = jnp.where(frame_valid[:, None], gated, 0.0).astype(jnp.bfloat16)
    padded = with_halo(gated, (("tm", 0),), KERNEL // 2)
    depthwise = jnp.zeros((frame_count, model_width), jnp.float32)
    for tap_index in range(KERNEL):
        depthwise = (
            depthwise
            + padded[tap_index : tap_index + frame_count].astype(jnp.float32) * dw_kernel[tap_index]
        )
    masked = jnp.where(frame_valid[:, None], depthwise, 0.0)
    first_moment, second_moment = lax.psum(
        (jnp.sum(masked, axis=0), jnp.sum(masked * depthwise, axis=0)), ("call", "tm")
    )
    count_all = jnp.sum(lengths).astype(jnp.float32)
    average = first_moment / count_all
    second = second_moment / count_all
    normal_act = (depthwise - average) * lax.rsqrt(
        second - average * average + 1e-05
    ) * bn_gain + bn_bias
    activated = normal_act * jax.nn.sigmoid(normal_act)
    conv_act = jnp.where(frame_valid[:, None], activated, 0.0).astype(jnp.bfloat16)
    return (attended[None], conv_act[None])


MESH = pl.DeviceIdType.MESH


def remote(source, target, send_sem, recv_sem, where):
    return pltpu.make_async_remote_copy(
        src_ref=source,
        dst_ref=target,
        send_sem=send_sem,
        recv_sem=recv_sem,
        device_id=where,
        device_id_type=MESH,
    )


def greet(places):
    barrier = pltpu.get_barrier_semaphore()
    for where in places:
        pl.semaphore_signal(barrier, inc=1, device_id=where, device_id_type=MESH)
    pl.semaphore_wait(barrier, len(places))


def gather_kernel(count, x_ref, w_ref, xall, wcol, send_x, recv_x, send_w, recv_w, own_sem):
    me = lax.axis_index("tm")
    y_peer = me + 2 - 4 * ((me // 2) % 2)
    c_peer = me + 1 - 2 * (me % 2)
    both = y_peer + 1 - 2 * (me % 2)
    greet([{"tm": (me + step) % count} for step in range(1, count)])
    own_x = pltpu.make_async_copy(x_ref, xall.at[me], own_sem.at[0])
    own_w = pltpu.make_async_copy(w_ref.at[me], wcol.at[me], own_sem.at[1])
    own_x.start()
    own_w.start()
    sends = []

    def push(source, owner, place):
        copy = remote(
            source, xall.at[owner], send_x.at[len(sends)], recv_x.at[owner], {"tm": place}
        )
        copy.start()
        sends.append(copy)

    def arrived(owner):
        remote(
            xall.at[owner], xall.at[owner], send_x.at[0], recv_x.at[owner], {"tm": c_peer}
        ).wait_recv()

    hops = range(4, count, 4)
    push(x_ref, me, y_peer)
    for hop in hops:
        push(x_ref, me, (me + hop) % count)
    push(x_ref, me, c_peer)
    w_sends = []
    for step in range(1, count):
        place = (me + step) % count
        copy = remote(
            w_ref.at[place], wcol.at[me], send_w.at[step], recv_w.at[me], {"tm": place}
        )
        copy.start()
        w_sends.append(copy)
    arrived(y_peer)
    push(xall.at[y_peer], y_peer, c_peer)
    for hop in hops:
        owner = (me + hop) % count
        arrived(owner)
        push(xall.at[owner], owner, y_peer)
        push(xall.at[owner], owner, c_peer)
    for hop in hops:
        owner = (y_peer + hop) % count
        arrived(owner)
        push(xall.at[owner], owner, c_peer)
    arrived(c_peer)
    arrived(both)
    for hop in hops:
        arrived((c_peer + hop) % count)
        arrived((both + hop) % count)
    for step in range(1, count):
        owner = (me + step) % count
        remote(
            w_ref.at[owner], wcol.at[owner], send_w.at[0], recv_w.at[owner], {"tm": c_peer}
        ).wait_recv()
    for copy in sends + w_sends:
        copy.wait_send()
    own_x.wait()
    own_w.wait()


def gather_call(normed, w_heads):
    count = w_heads.shape[0]
    anywhere = pl.BlockSpec(memory_space=pl.ANY)
    return pl.pallas_call(
        functools.partial(gather_kernel, count),
        out_shape=(
            jax.ShapeDtypeStruct((count,) + normed.shape, normed.dtype),
            jax.ShapeDtypeStruct(w_heads.shape, w_heads.dtype),
        ),
        in_specs=[anywhere] * 2,
        out_specs=(anywhere, anywhere),
        scratch_shapes=[
            pltpu.SemaphoreType.DMA((count,)),
            pltpu.SemaphoreType.DMA((count,)),
            pltpu.SemaphoreType.DMA((count,)),
            pltpu.SemaphoreType.DMA((count,)),
            pltpu.SemaphoreType.DMA((2,)),
        ],
        compiler_params=pltpu.CompilerParams(collective_id=0, has_side_effects=True),
        name="gather_frames",
    )(normed, w_heads)


def attend_kernel(scale, length_ref, q_ref, k_ref, v_ref, out_ref):
    block = pl.program_id(0)
    width = LEFT + SPAN
    first = pl.multiple_of(block * SPAN, SPAN)
    keys = k_ref[pl.ds(first, width), :]
    scores = lax.dot_general(
        q_ref[...], keys, (((1,), (1,)), ((), ())), preferred_element_type=jnp.float32
    )
    key_pos = block * SPAN - LEFT + lax.broadcasted_iota(jnp.int32, (SPAN, width), 1)
    query_pos = block * SPAN + lax.broadcasted_iota(jnp.int32, (SPAN, width), 0)
    allowed = (key_pos >= 0) & ((key_pos < length_ref[0]) | (key_pos == query_pos))
    raised = jnp.where(allowed, jnp.exp(scores * scale), 0.0)
    probs = (raised / jnp.sum(raised, axis=-1, keepdims=True)).astype(jnp.bfloat16)
    mixed = jnp.dot(probs, v_ref[pl.ds(first, width), :], preferred_element_type=jnp.float32)
    out_ref[0] = mixed.astype(jnp.bfloat16)


def attend_call(length, queries, keys, values):
    frames, width = queries.shape
    count = frames // SPAN
    whole = pl.BlockSpec((frames + LEFT, width), lambda i: (0, 0))
    return pl.pallas_call(
        functools.partial(attend_kernel, HEAD_DIM**-0.5),
        grid=(count,),
        out_shape=jax.ShapeDtypeStruct((count, SPAN, width), jnp.bfloat16),
        in_specs=[
            pl.BlockSpec(memory_space=pltpu.SMEM),
            pl.BlockSpec((SPAN, width), lambda i: (i, 0)),
            whole,
            whole,
        ],
        out_specs=pl.BlockSpec((1, SPAN, width), lambda i: (i, 0, 0)),
        compiler_params=pltpu.CompilerParams(vmem_limit_bytes=32 * 1024 * 1024),
        name="attend_head",
    )(length, queries, keys, values)


def exchange_kernel(count, x_ref, out_ref, send, recv, own_sem):
    me = lax.axis_index("tm")
    greet([{"tm": (me + step) % count} for step in range(1, count)])
    own = pltpu.make_async_copy(x_ref.at[me], out_ref.at[me], own_sem.at[0])
    own.start()
    sends = []
    for step in range(1, count):
        place = (me + step) % count
        copy = remote(x_ref.at[place], out_ref.at[me], send.at[step], recv.at[me], {"tm": place})
        copy.start()
        sends.append(copy)
    for step in range(1, count):
        owner = (me + step) % count
        remote(
            x_ref.at[owner], out_ref.at[owner], send.at[0], recv.at[owner], {"tm": owner}
        ).wait_recv()
    for copy in sends:
        copy.wait_send()
    own.wait()


def exchange_call(blocks):
    count = blocks.shape[0]
    anywhere = pl.BlockSpec(memory_space=pl.ANY)
    return pl.pallas_call(
        functools.partial(exchange_kernel, count),
        out_shape=jax.ShapeDtypeStruct(blocks.shape, blocks.dtype),
        in_specs=[anywhere],
        out_specs=anywhere,
        scratch_shapes=[
            pltpu.SemaphoreType.DMA((count,)),
            pltpu.SemaphoreType.DMA((count,)),
            pltpu.SemaphoreType.DMA((1,)),
        ],
        compiler_params=pltpu.CompilerParams(collective_id=1, has_side_effects=True),
        name="exchange_context",
    )(blocks)


EDGE = 16
STRIP = 128


def conv_kernel(
    count, g_ref, valid_ref, total_ref, taps_ref, gain_ref, bias_ref, out_ref,
    low, high, padded, depth, mine, plane, near, far,
    halo_send, halo_recv, near_send, near_recv, far_send, far_recv,
):
    me = lax.axis_index("tm")
    call = lax.axis_index("call")
    rows, width = depth.shape
    right, left = (me + 1) % count, (me + count - 1) % count
    peers = []
    for flips in range(1, 8):
        spot, side = me, call
        if flips & 1:
            spot = spot + 1 - 2 * (me % 2)
        if flips & 2:
            spot = spot + 2 - 4 * ((me // 2) % 2)
        if flips & 4:
            side = 1 - call
        peers.append({"call": side, "tm": spot})
    hops = [{"tm": (me + hop) % count} for hop in range(4, count, 4)]
    greet([{"tm": right}, {"tm": left}] + peers + hops)
    to_right = remote(
        g_ref.at[pl.ds(rows - EDGE, EDGE)], low, halo_send.at[0], halo_recv.at[0], {"tm": right}
    )
    to_left = remote(
        g_ref.at[pl.ds(0, EDGE)], high, halo_send.at[1], halo_recv.at[1], {"tm": left}
    )
    to_right.start()
    to_left.start()
    padded[EDGE : EDGE + rows, :] = g_ref[...].astype(jnp.float32)
    to_right.wait_recv()
    to_left.wait_recv()
    has_low = jnp.where(me > 0, 1.0, 0.0).astype(jnp.float32)
    has_high = jnp.where(me < count - 1, 1.0, 0.0).astype(jnp.float32)
    padded[0:EDGE, :] = low[...].astype(jnp.float32) * has_low
    padded[EDGE + rows : 2 * EDGE + rows, :] = high[...].astype(jnp.float32) * has_high
    valid = valid_ref[...]
    for at in range(0, width, STRIP):
        strip = slice(at, at + STRIP)
        total = jnp.zeros((rows, STRIP), jnp.float32)
        for tap in range(KERNEL):
            start = EDGE - KERNEL // 2 + tap
            total = total + padded[start : start + rows, strip] * taps_ref[tap : tap + 1, strip]
        depth[:, strip] = total
        masked = total * valid
        mine[0:1, strip] = jnp.sum(masked, axis=0, keepdims=True)
        mine[1:2, strip] = jnp.sum(masked * total, axis=0, keepdims=True)
    near_copies = []
    for slot, where in enumerate(peers):
        copy = remote(mine, near.at[slot], near_send.at[slot], near_recv.at[slot], where)
        copy.start()
        near_copies.append(copy)
    for copy in near_copies:
        copy.wait_recv()
    both = mine[...]
    for slot in range(len(peers)):
        both = both + near[slot]
    plane[...] = both
    far_copies = []
    for slot, where in enumerate(hops):
        copy = remote(plane, far.at[slot], far_send.at[slot], far_recv.at[slot], where)
        copy.start()
        far_copies.append(copy)
    for copy in far_copies:
        copy.wait_recv()
    for slot in range(len(hops)):
        both = both + far[slot]
    both = both / total_ref[...]
    average = both[0:1]
    spread = lax.rsqrt(both[1:2] - average * average + 1e-05)
    for at in range(0, width, STRIP):
        strip = slice(at, at + STRIP)
        act = (depth[:, strip] - average[:, strip]) * spread[:, strip]
        act = act * gain_ref[:, strip] + bias_ref[:, strip]
        act = act * jax.nn.sigmoid(act)
        out_ref[:, strip] = jnp.where(valid > 0.0, act, 0.0).astype(out_ref.dtype)
    for copy in [to_right, to_left] + near_copies + far_copies:
        copy.wait_send()


def conv_call(count, gated, valid, total, taps, gain, bias):
    rows, width = gated.shape
    vmem = pl.BlockSpec(memory_space=pltpu.VMEM)
    sems = pltpu.SemaphoreType.DMA
    far_count = count // 4 - 1
    return pl.pallas_call(
        functools.partial(conv_kernel, count),
        out_shape=jax.ShapeDtypeStruct(gated.shape, jnp.bfloat16),
        in_specs=[vmem] * 6,
        out_specs=vmem,
        scratch_shapes=[
            pltpu.VMEM((EDGE, width), jnp.bfloat16),
            pltpu.VMEM((EDGE, width), jnp.bfloat16),
            pltpu.VMEM((rows + 2 * EDGE, width), jnp.float32),
            pltpu.VMEM((rows, width), jnp.float32),
            pltpu.VMEM((2, width), jnp.float32),
            pltpu.VMEM((2, width), jnp.float32),
            pltpu.VMEM((7, 2, width), jnp.float32),
            pltpu.VMEM((far_count, 2, width), jnp.float32),
            sems((2,)), sems((2,)), sems((7,)), sems((7,)), sems((far_count,)), sems((far_count,)),
        ],
        compiler_params=pltpu.CompilerParams(
            collective_id=2, has_side_effects=True, vmem_limit_bytes=32 * 1024 * 1024
        ),
        name="conv_norm",
    )(gated, valid, total, taps, gain, bias)


def one_head_each(
    frames, lengths, ln_attn_gain, w_qkv, w_out, ln_conv_gain, w_pw1, dw_kernel, bn_gain, bn_bias
):
    stream = frames[0]
    frame_count, model_width = stream.shape
    count = lax.axis_size("tm")
    length = lax.dynamic_index_in_dim(lengths, lax.axis_index("call"), 0, keepdims=False)
    query_pos = lax.axis_index("tm") * frame_count + jnp.arange(frame_count, dtype=jnp.int32)
    frame_valid = (query_pos < length)[:, None]
    normed = layer_norm(stream, ln_attn_gain).astype(jnp.bfloat16)
    w_heads = w_qkv.reshape(-1, 3, count, HEAD_DIM).transpose(2, 0, 1, 3)
    w_heads = w_heads.reshape(count, -1, 3 * HEAD_DIM)
    all_frames, w_columns = gather_call(normed, w_heads)
    packed = contract_with(
        all_frames.reshape(-1, model_width), w_columns.reshape(model_width, -1)
    ).astype(jnp.bfloat16)
    queries = packed[:, :HEAD_DIM]
    keys = jnp.pad(packed[:, HEAD_DIM : 2 * HEAD_DIM], ((LEFT, 0), (0, 0)))
    values = jnp.pad(packed[:, 2 * HEAD_DIM :], ((LEFT, 0), (0, 0)))
    blocks = attend_call(length[None], queries, keys, values)
    context = exchange_call(blocks).transpose(1, 0, 2).reshape(frame_count, model_width)
    projected = contract_with(context, lax.all_gather(w_out, "tm", axis=0, tiled=True))
    attended = jnp.where(frame_valid, stream.astype(jnp.float32) + projected, 0.0).astype(
        jnp.bfloat16
    )
    conv_in = layer_norm(attended, ln_conv_gain).astype(jnp.bfloat16)
    expanded = contract_with(conv_in, lax.all_gather(w_pw1, "tm", axis=0, tiled=True))
    gated = expanded[:, :model_width] * jax.nn.sigmoid(expanded[:, model_width:])
    gated = jnp.where(frame_valid, gated, 0.0).astype(jnp.bfloat16)
    conv_act = conv_call(
        count,
        gated,
        frame_valid.astype(jnp.float32),
        jnp.sum(lengths).astype(jnp.float32).reshape(1, 1),
        dw_kernel,
        bn_gain[None],
        bn_bias[None],
    )
    return (attended[None], conv_act[None])


def fits_one_head(mesh):
    return mesh.shape["tm"] == 16 and mesh.shape["call"] == 2


def solution(mesh):
    return jax.shard_map(
        one_head_each if fits_one_head(mesh) else on_device,
        mesh=mesh,
        in_specs=(
            P("call", "tm", None),
            P(),
            P(),
            P("tm", None),
            P("tm", None),
            P(),
            P("tm", None),
            P(),
            P(),
            P(),
        ),
        out_specs=(P("call", "tm", None), P("call", "tm", None)),
        check_vma=False,
    )
```

```python
import functools

import jax
import jax.numpy as jnp
from jax import lax
from jax.experimental import pallas as pl
from jax.experimental.pallas import tpu as pltpu
from jax.sharding import PartitionSpec as P

HEAD_DIM = 64
SPAN = 128
LEFT = 1024
KERNEL = 9


def passed_along(value, axis, steps):
    count = lax.axis_size(axis)
    first, last = (max(0, -steps), min(count, count - steps))
    return lax.ppermute(value, axis, [(source, source + steps) for source in range(first, last)])


def with_halo(cells, sides, width):
    for axis, dim in sides:
        count = lax.axis_size(axis)
        ends = count - 1
        head = lax.slice_in_dim(cells, 0, width, axis=dim)
        tail = lax.slice_in_dim(cells, cells.shape[dim] - width, cells.shape[dim], axis=dim)
        cells = jnp.concatenate(
            [
                lax.ppermute(tail, axis, [(i, (i + 1) % count) for i in range(ends)]),
                cells,
                lax.ppermute(head, axis, [((i + 1) % count, i) for i in range(ends)]),
            ],
            axis=dim,
        )
    return cells


def layer_norm(values, gain_vec):
    wide = values.astype(jnp.float32)
    center = wide - jnp.mean(wide, axis=-1, keepdims=True)
    spread = jnp.mean(center * center, axis=-1, keepdims=True)
    return center * lax.rsqrt(spread + 1e-05) * gain_vec


def contract_with(left, rows_piece):
    return jnp.dot(left, rows_piece, preferred_element_type=jnp.float32)


def on_device(
    frames, lengths, ln_attn_gain, w_qkv, w_out, ln_conv_gain, w_pw1, dw_kernel, bn_gain, bn_bias
):
    stream = frames[0]
    frame_count, model_width = stream.shape
    head_count = model_width // HEAD_DIM
    length = lax.dynamic_index_in_dim(lengths, lax.axis_index("call"), 0, keepdims=False)
    first_row = lax.axis_index("tm") * frame_count
    query_pos = first_row + jnp.arange(frame_count, dtype=jnp.int32)
    frame_valid = query_pos < length
    normed = layer_norm(stream, ln_attn_gain).astype(jnp.bfloat16)
    prior_blocks = LEFT // frame_count
    packed = contract_with(normed, lax.all_gather(w_qkv, "tm", axis=0, tiled=True))
    queries = packed[:, :model_width].astype(jnp.bfloat16)
    key_value = jnp.stack(
        [
            packed[:, model_width : 2 * model_width].astype(jnp.bfloat16),
            packed[:, 2 * model_width :].astype(jnp.bfloat16),
        ]
    )
    blocks = []
    current = key_value
    for hop_index in range(prior_blocks):
        current = passed_along(current, "tm", 1)
        blocks.append(current)
    context_kv = jnp.concatenate(blocks[::-1] + [key_value], axis=1)
    key_count = context_kv.shape[1]
    key_pos = first_row - prior_blocks * frame_count + jnp.arange(key_count, dtype=jnp.int32)
    span_first = query_pos // SPAN * SPAN
    allowed = (key_pos[None, :] >= 0) & (key_pos[None, :] >= span_first[:, None] - LEFT)
    allowed = allowed & (key_pos[None, :] < span_first[:, None] + SPAN)
    allowed = allowed & ((key_pos[None, :] < length) | (key_pos[None, :] == query_pos[:, None]))
    group_size = 4
    group_count = head_count // group_size
    query_groups = queries.reshape(frame_count, group_count, group_size, HEAD_DIM).transpose(
        1, 0, 2, 3
    )
    key_groups = (
        context_kv[0].reshape(key_count, group_count, group_size, HEAD_DIM).transpose(1, 0, 2, 3)
    )
    value_groups = (
        context_kv[1].reshape(key_count, group_count, group_size, HEAD_DIM).transpose(1, 0, 2, 3)
    )
    scale_factor = 1.0 / jnp.sqrt(jnp.float32(HEAD_DIM))

    def attend_group(operands):
        query_part, key_part, value_part = operands
        scores = (
            jnp.einsum("qhd,khd->hqk", query_part, key_part, preferred_element_type=jnp.float32)
            * scale_factor
        )
        raised = jnp.where(allowed[None], jnp.exp(scores), 0.0)
        probs = (raised / jnp.sum(raised, axis=-1, keepdims=True)).astype(jnp.bfloat16)
        mixed = jnp.einsum("hqk,khd->qhd", probs, value_part, preferred_element_type=jnp.float32)
        return mixed.astype(jnp.bfloat16)

    context = lax.map(attend_group, (query_groups, key_groups, value_groups))
    context = context.transpose(1, 0, 2, 3).reshape(frame_count, model_width)
    projected = contract_with(context, lax.all_gather(w_out, "tm", axis=0, tiled=True))
    attended = jnp.where(frame_valid[:, None], stream.astype(jnp.float32) + projected, 0.0).astype(
        jnp.bfloat16
    )
    conv_in = layer_norm(attended, ln_conv_gain).astype(jnp.bfloat16)
    expanded = contract_with(conv_in, lax.all_gather(w_pw1, "tm", axis=0, tiled=True))
    gated = expanded[:, :model_width] * jax.nn.sigmoid(expanded[:, model_width:])
    gated = jnp.where(frame_valid[:, None], gated, 0.0).astype(jnp.bfloat16)
    padded = with_halo(gated, (("tm", 0),), KERNEL // 2)
    depthwise = jnp.zeros((frame_count, model_width), jnp.float32)
    for tap_index in range(KERNEL):
        depthwise = (
            depthwise
            + padded[tap_index : tap_index + frame_count].astype(jnp.float32) * dw_kernel[tap_index]
        )
    masked = jnp.where(frame_valid[:, None], depthwise, 0.0)
    first_moment, second_moment = lax.psum(
        (jnp.sum(masked, axis=0), jnp.sum(masked * depthwise, axis=0)), ("call", "tm")
    )
    count_all = jnp.sum(lengths).astype(jnp.float32)
    average = first_moment / count_all
    second = second_moment / count_all
    normal_act = (depthwise - average) * lax.rsqrt(
        second - average * average + 1e-05
    ) * bn_gain + bn_bias
    activated = normal_act * jax.nn.sigmoid(normal_act)
    conv_act = jnp.where(frame_valid[:, None], activated, 0.0).astype(jnp.bfloat16)
    return (attended[None], conv_act[None])


MESH = pl.DeviceIdType.MESH


def remote(source, target, send_sem, recv_sem, where):
    return pltpu.make_async_remote_copy(
        src_ref=source,
        dst_ref=target,
        send_sem=send_sem,
        recv_sem=recv_sem,
        device_id=where,
        device_id_type=MESH,
    )


def greet(places):
    barrier = pltpu.get_barrier_semaphore()
    for where in places:
        pl.semaphore_signal(barrier, inc=1, device_id=where, device_id_type=MESH)
    pl.semaphore_wait(barrier, len(places))


def gather_kernel(
    count, stream_ref, gain_ref, rows_ref, xall, wcol, x_ref, w_ref,
    send_x, recv_x, send_w, recv_w, own_sem,
):
    me = lax.axis_index("tm")
    y_peer = me + 2 - 4 * ((me // 2) % 2)
    c_peer = me + 1 - 2 * (me % 2)
    both = y_peer + 1 - 2 * (me % 2)
    x_ref[...] = layer_norm(stream_ref[...], gain_ref[...]).astype(jnp.bfloat16)
    width = rows_ref.shape[1] // 3
    for head in range(count):
        for part in range(3):
            start = part * width + head * HEAD_DIM
            w_ref[head, :, part * HEAD_DIM : (part + 1) * HEAD_DIM] = rows_ref[
                :, start : start + HEAD_DIM
            ]
    greet([{"tm": (me + step) % count} for step in range(1, count)])
    own_x = pltpu.make_async_copy(x_ref, xall.at[me], own_sem.at[0])
    own_w = pltpu.make_async_copy(w_ref.at[me], wcol.at[me], own_sem.at[1])
    own_x.start()
    own_w.start()
    sends = []

    def push(source, owner, place):
        copy = remote(
            source, xall.at[owner], send_x.at[len(sends)], recv_x.at[owner], {"tm": place}
        )
        copy.start()
        sends.append(copy)

    def arrived(owner):
        remote(
            xall.at[owner], xall.at[owner], send_x.at[0], recv_x.at[owner], {"tm": c_peer}
        ).wait_recv()

    hops = range(4, count, 4)
    push(x_ref, me, y_peer)
    for hop in hops:
        push(x_ref, me, (me + hop) % count)
    push(x_ref, me, c_peer)
    w_sends = []
    for step in range(1, count):
        place = (me + step) % count
        copy = remote(
            w_ref.at[place], wcol.at[me], send_w.at[step], recv_w.at[me], {"tm": place}
        )
        copy.start()
        w_sends.append(copy)
    arrived(y_peer)
    push(xall.at[y_peer], y_peer, c_peer)
    for hop in hops:
        owner = (me + hop) % count
        arrived(owner)
        push(xall.at[owner], owner, y_peer)
        push(xall.at[owner], owner, c_peer)
    for hop in hops:
        owner = (y_peer + hop) % count
        arrived(owner)
        push(xall.at[owner], owner, c_peer)
    arrived(c_peer)
    arrived(both)
    for hop in hops:
        arrived((c_peer + hop) % count)
        arrived((both + hop) % count)
    for step in range(1, count):
        owner = (me + step) % count
        remote(
            w_ref.at[owner], wcol.at[owner], send_w.at[0], recv_w.at[owner], {"tm": c_peer}
        ).wait_recv()
    for copy in sends + w_sends:
        copy.wait_send()
    own_x.wait()
    own_w.wait()


def gather_call(stream, gain, w_rows):
    count = lax.axis_size("tm")
    depth = w_rows.shape[0]
    heads = (count, depth, 3 * HEAD_DIM)
    anywhere = pl.BlockSpec(memory_space=pl.ANY)
    vmem = pl.BlockSpec(memory_space=pltpu.VMEM)
    sems = pltpu.SemaphoreType.DMA
    return pl.pallas_call(
        functools.partial(gather_kernel, count),
        out_shape=(
            jax.ShapeDtypeStruct((count,) + stream.shape, jnp.bfloat16),
            jax.ShapeDtypeStruct(heads, jnp.bfloat16),
        ),
        in_specs=[vmem] * 3,
        out_specs=(anywhere, anywhere),
        scratch_shapes=[
            pltpu.VMEM(stream.shape, jnp.bfloat16),
            pltpu.VMEM(heads, jnp.bfloat16),
            sems((count,)), sems((count,)), sems((count,)), sems((count,)), sems((2,)),
        ],
        compiler_params=pltpu.CompilerParams(
            collective_id=0, has_side_effects=True, vmem_limit_bytes=24 * 1024 * 1024
        ),
        name="gather_frames",
    )(stream, gain, w_rows)


def attend_kernel(
    count, scale, length_ref, q_ref, k_ref, v_ref, rows_ref, out_ref, wall,
    mixed_ref, landed, send_c, recv_c, send_w, recv_w, own_sem,
):
    me = lax.axis_index("tm")
    call = lax.axis_index("call")
    y_peer = me + 2 - 4 * ((me // 2) % 2)
    c_peer = me + 1 - 2 * (me % 2)
    twin = {"call": 1 - call, "tm": me}
    greet([{"tm": (me + step) % count} for step in range(1, count)] + [twin])
    sends = []

    def push(source, part, owner, where):
        copy = remote(
            source, wall.at[part, owner], send_w.at[len(sends)], recv_w.at[part, owner], where
        )
        copy.start()
        sends.append(copy)

    def arrived(part, owner):
        remote(
            wall.at[part, owner], wall.at[part, owner], send_w.at[0], recv_w.at[part, owner],
            {"tm": c_peer},
        ).wait_recv()

    def relay(part, owner, places):
        arrived(part, owner)
        for where in places:
            push(wall.at[part, owner], part, owner, where)

    width = LEFT + SPAN
    length = length_ref[call]

    def attend(block):
        first = pl.multiple_of(block * SPAN, SPAN)
        scores = lax.dot_general(
            q_ref[pl.ds(first, SPAN), :],
            k_ref[pl.ds(first, width), :],
            (((1,), (1,)), ((), ())),
            preferred_element_type=jnp.float32,
        )
        key_pos = block * SPAN - LEFT + lax.broadcasted_iota(jnp.int32, (SPAN, width), 1)
        query_pos = block * SPAN + lax.broadcasted_iota(jnp.int32, (SPAN, width), 0)
        allowed = (key_pos >= 0) & ((key_pos < length) | (key_pos == query_pos))
        raised = jnp.where(allowed, jnp.exp(scores * scale), 0.0)
        probs = (raised / jnp.sum(raised, axis=-1, keepdims=True)).astype(jnp.bfloat16)
        mixed = jnp.dot(probs, v_ref[pl.ds(first, width), :], preferred_element_type=jnp.float32)
        return mixed.astype(jnp.bfloat16)

    def attend_and_send(step, carry):
        place = (me + step) % count
        mixed_ref[place] = attend(place)
        remote(
            mixed_ref.at[place], landed.at[me], send_c.at[place], recv_c.at[me], {"tm": place}
        ).start()
        return carry

    hops = range(4, count, 4)
    own = pltpu.make_async_copy(rows_ref, wall.at[:, me], own_sem.at[0])
    own.start()
    for hop in hops:
        for part in (call, 2):
            push(rows_ref.at[part], part, me, {"tm": (me + hop) % count})
    for part in (call, 2):
        push(rows_ref.at[part], part, me, {"tm": y_peer})
    for part in range(3):
        push(rows_ref.at[part], part, me, {"tm": c_peer})
    lax.fori_loop(1, count // 2, attend_and_send, 0)
    relay(call, y_peer, [twin, {"tm": c_peer}])
    relay(2, y_peer, [{"tm": c_peer}])
    relay(call, (me + 4) % count, [{"tm": y_peer}, twin, {"tm": c_peer}])
    relay(2, (me + 4) % count, [{"tm": y_peer}, {"tm": c_peer}])
    lax.fori_loop(count // 2, count, attend_and_send, 0)
    landed[me] = attend(me)
    for hop in range(8, count, 4):
        owner = (me + hop) % count
        relay(call, owner, [{"tm": y_peer}, twin, {"tm": c_peer}])
        relay(2, owner, [{"tm": y_peer}, {"tm": c_peer}])
    for hop in hops:
        owner = (y_peer + hop) % count
        relay(call, owner, [twin, {"tm": c_peer}])
        relay(2, owner, [{"tm": c_peer}])
    relay(1 - call, y_peer, [{"tm": c_peer}])
    for hop in hops:
        relay(1 - call, (me + hop) % count, [{"tm": c_peer}])
        relay(1 - call, (y_peer + hop) % count, [{"tm": c_peer}])
    for step in range(1, count):
        owner = (me + step) % count
        remote(
            mixed_ref.at[owner], landed.at[owner], send_c.at[owner], recv_c.at[owner],
            {"tm": owner},
        ).wait()
    for pair in range(0, count, 2):
        out_ref[:, pair * HEAD_DIM : (pair + 2) * HEAD_DIM] = jnp.concatenate(
            [landed[pair], landed[pair + 1]], axis=1
        )
    own.wait()
    both = c_peer + 2 - 4 * ((me // 2) % 2)
    for part in range(3):
        for hop in range(0, count, 4):
            arrived(part, (c_peer + hop) % count)
            arrived(part, (both + hop) % count)
    for copy in sends:
        copy.wait_send()


def attend_call(lengths, queries, keys, values, rows):
    frames, width = queries.shape
    count = frames // SPAN
    anywhere = pl.BlockSpec(memory_space=pl.ANY)
    vmem = pl.BlockSpec(memory_space=pltpu.VMEM)
    sems = pltpu.SemaphoreType.DMA
    parts, depth, columns = rows.shape
    copies = 2 * (count // 4 - 1) + 5 + 3 + 5 * (count // 4 - 1) + 3 * (count // 4 - 1) + 7
    return pl.pallas_call(
        functools.partial(attend_kernel, count, HEAD_DIM**-0.5),
        out_shape=(
            jax.ShapeDtypeStruct((SPAN, count * width), jnp.bfloat16),
            jax.ShapeDtypeStruct((parts, count, depth, columns), jnp.bfloat16),
        ),
        in_specs=[pl.BlockSpec(memory_space=pltpu.SMEM), vmem, vmem, vmem, anywhere],
        out_specs=(vmem, anywhere),
        scratch_shapes=[
            pltpu.VMEM((count, SPAN, width), jnp.bfloat16),
            pltpu.VMEM((count, SPAN, width), jnp.bfloat16),
            sems((count,)), sems((count,)), sems((copies,)), sems((parts, count)), sems((1,)),
        ],
        compiler_params=pltpu.CompilerParams(
            collective_id=1, has_side_effects=True, vmem_limit_bytes=32 * 1024 * 1024
        ),
        name="attend_exchange",
    )(lengths, queries, keys, values, rows)


def project_kernel(length_ref, context_ref, stream_ref, w_ref, gain_ref, attended_ref, gated_ref):
    rows = stream_ref.shape[0]
    first = lax.axis_index("tm") * rows
    length = length_ref[lax.axis_index("call")]
    valid = first + lax.broadcasted_iota(jnp.int32, (rows, 1), 0) < length
    wide = stream_ref[...].astype(jnp.float32) + contract_with(context_ref[...], w_ref[0])
    attended = jnp.where(valid, wide, 0.0).astype(jnp.bfloat16)
    attended_ref[...] = attended
    conv_in = layer_norm(attended, gain_ref[...]).astype(jnp.bfloat16)
    gated = contract_with(conv_in, w_ref[1]) * jax.nn.sigmoid(contract_with(conv_in, w_ref[2]))
    gated_ref[...] = jnp.where(valid, gated, 0.0).astype(jnp.bfloat16)


def project_call(lengths, context, stream, weights, gain):
    vmem = pl.BlockSpec(memory_space=pltpu.VMEM)
    return pl.pallas_call(
        project_kernel,
        out_shape=(jax.ShapeDtypeStruct(stream.shape, jnp.bfloat16),) * 2,
        in_specs=[pl.BlockSpec(memory_space=pltpu.SMEM)] + [vmem] * 4,
        out_specs=(vmem, vmem),
        compiler_params=pltpu.CompilerParams(vmem_limit_bytes=32 * 1024 * 1024),
        name="project_gate",
    )(lengths, context, stream, weights, gain)


EDGE = 16
STRIP = 128


def conv_kernel(
    count, length_ref, g_ref, taps_ref, gain_ref, bias_ref, out_ref,
    low, high, padded, depth, mine, plane, near, far,
    halo_send, halo_recv, near_send, near_recv, far_send, far_recv,
):
    me = lax.axis_index("tm")
    call = lax.axis_index("call")
    rows, width = depth.shape
    right, left = (me + 1) % count, (me + count - 1) % count
    peers = []
    for flips in range(1, 8):
        spot, side = me, call
        if flips & 1:
            spot = spot + 1 - 2 * (me % 2)
        if flips & 2:
            spot = spot + 2 - 4 * ((me // 2) % 2)
        if flips & 4:
            side = 1 - call
        peers.append({"call": side, "tm": spot})
    hops = [{"tm": (me + hop) % count} for hop in range(4, count, 4)]
    greet([{"tm": right}, {"tm": left}] + peers + hops)
    to_right = remote(
        g_ref.at[pl.ds(rows - EDGE, EDGE)], low, halo_send.at[0], halo_recv.at[0], {"tm": right}
    )
    to_left = remote(
        g_ref.at[pl.ds(0, EDGE)], high, halo_send.at[1], halo_recv.at[1], {"tm": left}
    )
    to_right.start()
    to_left.start()
    padded[EDGE : EDGE + rows, :] = g_ref[...].astype(jnp.float32)
    to_right.wait_recv()
    to_left.wait_recv()
    has_low = jnp.where(me > 0, 1.0, 0.0).astype(jnp.float32)
    has_high = jnp.where(me < count - 1, 1.0, 0.0).astype(jnp.float32)
    padded[0:EDGE, :] = low[...].astype(jnp.float32) * has_low
    padded[EDGE + rows : 2 * EDGE + rows, :] = high[...].astype(jnp.float32) * has_high
    first = me * rows + lax.broadcasted_iota(jnp.int32, (rows, 1), 0)
    valid = jnp.where(first < length_ref[call], 1.0, 0.0).astype(jnp.float32)
    for at in range(0, width, STRIP):
        strip = slice(at, at + STRIP)
        total = jnp.zeros((rows, STRIP), jnp.float32)
        for tap in range(KERNEL):
            start = EDGE - KERNEL // 2 + tap
            total = total + padded[start : start + rows, strip] * taps_ref[tap : tap + 1, strip]
        depth[:, strip] = total
        masked = total * valid
        mine[0:1, strip] = jnp.sum(masked, axis=0, keepdims=True)
        mine[1:2, strip] = jnp.sum(masked * total, axis=0, keepdims=True)
    near_copies = []
    for slot, where in enumerate(peers):
        copy = remote(mine, near.at[slot], near_send.at[slot], near_recv.at[slot], where)
        copy.start()
        near_copies.append(copy)
    for copy in near_copies:
        copy.wait_recv()
    both = mine[...]
    for slot in range(len(peers)):
        both = both + near[slot]
    plane[...] = both
    far_copies = []
    for slot, where in enumerate(hops):
        copy = remote(plane, far.at[slot], far_send.at[slot], far_recv.at[slot], where)
        copy.start()
        far_copies.append(copy)
    for copy in far_copies:
        copy.wait_recv()
    for slot in range(len(hops)):
        both = both + far[slot]
    both = both / (length_ref[0] + length_ref[1]).astype(jnp.float32)
    average = both[0:1]
    spread = lax.rsqrt(both[1:2] - average * average + 1e-05)
    for at in range(0, width, STRIP):
        strip = slice(at, at + STRIP)
        act = (depth[:, strip] - average[:, strip]) * spread[:, strip]
        act = act * gain_ref[:, strip] + bias_ref[:, strip]
        act = act * jax.nn.sigmoid(act)
        out_ref[:, strip] = jnp.where(valid > 0.0, act, 0.0).astype(out_ref.dtype)
    for copy in [to_right, to_left] + near_copies + far_copies:
        copy.wait_send()


def conv_call(count, lengths, gated, taps, gain, bias):
    rows, width = gated.shape
    vmem = pl.BlockSpec(memory_space=pltpu.VMEM)
    sems = pltpu.SemaphoreType.DMA
    far_count = count // 4 - 1
    return pl.pallas_call(
        functools.partial(conv_kernel, count),
        out_shape=jax.ShapeDtypeStruct(gated.shape, jnp.bfloat16),
        in_specs=[pl.BlockSpec(memory_space=pltpu.SMEM)] + [vmem] * 4,
        out_specs=vmem,
        scratch_shapes=[
            pltpu.VMEM((EDGE, width), jnp.bfloat16),
            pltpu.VMEM((EDGE, width), jnp.bfloat16),
            pltpu.VMEM((rows + 2 * EDGE, width), jnp.float32),
            pltpu.VMEM((rows, width), jnp.float32),
            pltpu.VMEM((2, width), jnp.float32),
            pltpu.VMEM((2, width), jnp.float32),
            pltpu.VMEM((7, 2, width), jnp.float32),
            pltpu.VMEM((far_count, 2, width), jnp.float32),
            sems((2,)), sems((2,)), sems((7,)), sems((7,)), sems((far_count,)), sems((far_count,)),
        ],
        compiler_params=pltpu.CompilerParams(
            collective_id=2, has_side_effects=True, vmem_limit_bytes=32 * 1024 * 1024
        ),
        name="conv_norm",
    )(lengths, gated, taps, gain, bias)


def one_head_each(
    frames, lengths, ln_attn_gain, w_qkv, w_out, ln_conv_gain, w_pw1, dw_kernel, bn_gain, bn_bias
):
    stream = frames[0]
    model_width = stream.shape[1]
    count = lax.axis_size("tm")
    all_frames, w_columns = gather_call(stream, ln_attn_gain[None], w_qkv)
    packed = contract_with(
        all_frames.reshape(-1, model_width), w_columns.reshape(model_width, -1)
    ).astype(jnp.bfloat16)
    queries = packed[:, :HEAD_DIM]
    keys = jnp.pad(packed[:, HEAD_DIM : 2 * HEAD_DIM], ((LEFT, 0), (0, 0)))
    values = jnp.pad(packed[:, 2 * HEAD_DIM :], ((LEFT, 0), (0, 0)))
    rows = jnp.stack([w_out, w_pw1[:, :model_width], w_pw1[:, model_width:]])
    context, weights = attend_call(lengths, queries, keys, values, rows)
    weights = weights.reshape(3, model_width, model_width)
    attended, gated = project_call(lengths, context, stream, weights, ln_conv_gain[None])
    conv_act = conv_call(count, lengths, gated, dw_kernel, bn_gain[None], bn_bias[None])
    return (attended[None], conv_act[None])


def fits_one_head(mesh):
    return mesh.shape["tm"] == 16 and mesh.shape["call"] == 2


def solution(mesh):
    return jax.shard_map(
        one_head_each if fits_one_head(mesh) else on_device,
        mesh=mesh,
        in_specs=(
            P("call", "tm", None),
            P(),
            P(),
            P("tm", None),
            P("tm", None),
            P(),
            P("tm", None),
            P(),
            P(),
            P(),
        ),
        out_specs=(P("call", "tm", None), P("call", "tm", None)),
        check_vma=False,
    )
```

```python
import functools

import jax
import jax.numpy as jnp
from jax import lax
from jax.experimental import pallas as pl
from jax.experimental.pallas import tpu as pltpu
from jax.sharding import PartitionSpec as P

HEAD_DIM = 64
SPAN = 128
LEFT = 1024
KERNEL = 9


def passed_along(value, axis, steps):
    count = lax.axis_size(axis)
    first, last = (max(0, -steps), min(count, count - steps))
    return lax.ppermute(value, axis, [(source, source + steps) for source in range(first, last)])


def with_halo(cells, sides, width):
    for axis, dim in sides:
        count = lax.axis_size(axis)
        ends = count - 1
        head = lax.slice_in_dim(cells, 0, width, axis=dim)
        tail = lax.slice_in_dim(cells, cells.shape[dim] - width, cells.shape[dim], axis=dim)
        cells = jnp.concatenate(
            [
                lax.ppermute(tail, axis, [(i, (i + 1) % count) for i in range(ends)]),
                cells,
                lax.ppermute(head, axis, [((i + 1) % count, i) for i in range(ends)]),
            ],
            axis=dim,
        )
    return cells


def layer_norm(values, gain_vec):
    wide = values.astype(jnp.float32)
    center = wide - jnp.mean(wide, axis=-1, keepdims=True)
    spread = jnp.mean(center * center, axis=-1, keepdims=True)
    return center * lax.rsqrt(spread + 1e-05) * gain_vec


def contract_with(left, rows_piece):
    return jnp.dot(left, rows_piece, preferred_element_type=jnp.float32)


def on_device(
    frames, lengths, ln_attn_gain, w_qkv, w_out, ln_conv_gain, w_pw1, dw_kernel, bn_gain, bn_bias
):
    stream = frames[0]
    frame_count, model_width = stream.shape
    head_count = model_width // HEAD_DIM
    length = lax.dynamic_index_in_dim(lengths, lax.axis_index("call"), 0, keepdims=False)
    first_row = lax.axis_index("tm") * frame_count
    query_pos = first_row + jnp.arange(frame_count, dtype=jnp.int32)
    frame_valid = query_pos < length
    normed = layer_norm(stream, ln_attn_gain).astype(jnp.bfloat16)
    prior_blocks = LEFT // frame_count
    packed = contract_with(normed, lax.all_gather(w_qkv, "tm", axis=0, tiled=True))
    queries = packed[:, :model_width].astype(jnp.bfloat16)
    key_value = jnp.stack(
        [
            packed[:, model_width : 2 * model_width].astype(jnp.bfloat16),
            packed[:, 2 * model_width :].astype(jnp.bfloat16),
        ]
    )
    blocks = []
    current = key_value
    for hop_index in range(prior_blocks):
        current = passed_along(current, "tm", 1)
        blocks.append(current)
    context_kv = jnp.concatenate(blocks[::-1] + [key_value], axis=1)
    key_count = context_kv.shape[1]
    key_pos = first_row - prior_blocks * frame_count + jnp.arange(key_count, dtype=jnp.int32)
    span_first = query_pos // SPAN * SPAN
    allowed = (key_pos[None, :] >= 0) & (key_pos[None, :] >= span_first[:, None] - LEFT)
    allowed = allowed & (key_pos[None, :] < span_first[:, None] + SPAN)
    allowed = allowed & ((key_pos[None, :] < length) | (key_pos[None, :] == query_pos[:, None]))
    group_size = 4
    group_count = head_count // group_size
    query_groups = queries.reshape(frame_count, group_count, group_size, HEAD_DIM).transpose(
        1, 0, 2, 3
    )
    key_groups = (
        context_kv[0].reshape(key_count, group_count, group_size, HEAD_DIM).transpose(1, 0, 2, 3)
    )
    value_groups = (
        context_kv[1].reshape(key_count, group_count, group_size, HEAD_DIM).transpose(1, 0, 2, 3)
    )
    scale_factor = 1.0 / jnp.sqrt(jnp.float32(HEAD_DIM))

    def attend_group(operands):
        query_part, key_part, value_part = operands
        scores = (
            jnp.einsum("qhd,khd->hqk", query_part, key_part, preferred_element_type=jnp.float32)
            * scale_factor
        )
        raised = jnp.where(allowed[None], jnp.exp(scores), 0.0)
        probs = (raised / jnp.sum(raised, axis=-1, keepdims=True)).astype(jnp.bfloat16)
        mixed = jnp.einsum("hqk,khd->qhd", probs, value_part, preferred_element_type=jnp.float32)
        return mixed.astype(jnp.bfloat16)

    context = lax.map(attend_group, (query_groups, key_groups, value_groups))
    context = context.transpose(1, 0, 2, 3).reshape(frame_count, model_width)
    projected = contract_with(context, lax.all_gather(w_out, "tm", axis=0, tiled=True))
    attended = jnp.where(frame_valid[:, None], stream.astype(jnp.float32) + projected, 0.0).astype(
        jnp.bfloat16
    )
    conv_in = layer_norm(attended, ln_conv_gain).astype(jnp.bfloat16)
    expanded = contract_with(conv_in, lax.all_gather(w_pw1, "tm", axis=0, tiled=True))
    gated = expanded[:, :model_width] * jax.nn.sigmoid(expanded[:, model_width:])
    gated = jnp.where(frame_valid[:, None], gated, 0.0).astype(jnp.bfloat16)
    padded = with_halo(gated, (("tm", 0),), KERNEL // 2)
    depthwise = jnp.zeros((frame_count, model_width), jnp.float32)
    for tap_index in range(KERNEL):
        depthwise = (
            depthwise
            + padded[tap_index : tap_index + frame_count].astype(jnp.float32) * dw_kernel[tap_index]
        )
    masked = jnp.where(frame_valid[:, None], depthwise, 0.0)
    first_moment, second_moment = lax.psum(
        (jnp.sum(masked, axis=0), jnp.sum(masked * depthwise, axis=0)), ("call", "tm")
    )
    count_all = jnp.sum(lengths).astype(jnp.float32)
    average = first_moment / count_all
    second = second_moment / count_all
    normal_act = (depthwise - average) * lax.rsqrt(
        second - average * average + 1e-05
    ) * bn_gain + bn_bias
    activated = normal_act * jax.nn.sigmoid(normal_act)
    conv_act = jnp.where(frame_valid[:, None], activated, 0.0).astype(jnp.bfloat16)
    return (attended[None], conv_act[None])


MESH = pl.DeviceIdType.MESH


def remote(source, target, send_sem, recv_sem, where):
    return pltpu.make_async_remote_copy(
        src_ref=source,
        dst_ref=target,
        send_sem=send_sem,
        recv_sem=recv_sem,
        device_id=where,
        device_id_type=MESH,
    )


def greet(places):
    barrier = pltpu.get_barrier_semaphore()
    for where in places:
        pl.semaphore_signal(barrier, inc=1, device_id=where, device_id_type=MESH)
    pl.semaphore_wait(barrier, len(places))


class Relay:
    def __init__(self, count, buffer, sems):
        self.count = count
        self.buffer = buffer
        self.up, self.down, self.over, self.across, self.landed = sems
        self.me = lax.axis_index("tm")
        self.planes = count // 4
        self.plane = self.me // 4
        self.y_peer = self.me + 2 - 4 * ((self.me // 2) % 2)
        self.c_peer = self.me + 1 - 2 * (self.me % 2)

    def copy(self, source, part, owner, send, place):
        return remote(
            source,
            self.buffer.at[part, owner],
            send.at[part, owner],
            self.landed.at[part, owner],
            {"tm": place % self.count},
        )

    def held(self, part, owner):
        return self.buffer.at[part, owner]

    def arrived(self, part, owner):
        self.copy(self.held(part, owner), part, owner, self.across, self.c_peer).wait_recv()

    def start(self, source, part):
        me = self.me

        @pl.when(self.plane < self.planes - 1)
        def _():
            self.copy(source, part, me, self.up, me + 4).start()

        @pl.when(self.plane > 0)
        def _():
            self.copy(source, part, me, self.down, me + self.count - 4).start()

        self.copy(source, part, me, self.over, self.y_peer).start()

    def start_across(self, source, part):
        self.copy(source, part, self.me, self.across, self.c_peer).start()

    def step(self, at, part, extra=None):
        me = self.me
        far = 4 * (at + 1)

        @pl.when(self.plane > at)
        def _():
            owner = me - far
            self.arrived(part, owner)
            held = self.held(part, owner)

            @pl.when(self.plane < self.planes - 1)
            def _():
                self.copy(held, part, owner, self.up, me + 4).start()

            self.copy(held, part, owner, self.over, self.y_peer).start()
            if extra is not None:
                extra(part, owner)
            self.copy(held, part, owner, self.across, self.c_peer).start()

        @pl.when(self.plane + at + 1 < self.planes)
        def _():
            owner = me + far
            self.arrived(part, owner)
            held = self.held(part, owner)

            @pl.when(self.plane > 0)
            def _():
                self.copy(held, part, owner, self.down, me + self.count - 4).start()

            self.copy(held, part, owner, self.over, self.y_peer).start()
            if extra is not None:
                extra(part, owner)
            self.copy(held, part, owner, self.across, self.c_peer).start()

    def pass_across(self, part, owner, extra=None):
        self.arrived(part, owner)
        if extra is not None:
            extra(part, owner)
        self.copy(self.held(part, owner), part, owner, self.across, self.c_peer).start()

    def step_over(self, at, part, extra=None):
        if at < 0:
            self.pass_across(part, self.y_peer, extra)
            return
        far = 4 * (at + 1)

        @pl.when(self.plane > at)
        def _():
            self.pass_across(part, self.y_peer - far, extra)

        @pl.when(self.plane + at + 1 < self.planes)
        def _():
            self.pass_across(part, self.y_peer + far, extra)

    def column(self, base):
        return [(base + hop) % self.count for hop in range(0, self.count, 4)]

    def receive_across(self, part):
        both = self.c_peer + self.y_peer - self.me
        for owner in self.column(self.c_peer) + self.column(both):
            self.arrived(part, owner)

    def finish_sends(self, part):
        me = self.me
        for owner in self.column(me):
            plane = owner // 4

            @pl.when((plane <= self.plane) & (self.plane < self.planes - 1))
            def _():
                self.copy(self.held(part, owner), part, owner, self.up, me + 4).wait_send()

            @pl.when((plane >= self.plane) & (self.plane > 0))
            def _():
                place = me + self.count - 4
                self.copy(self.held(part, owner), part, owner, self.down, place).wait_send()

            self.copy(self.held(part, owner), part, owner, self.over, self.y_peer).wait_send()
        for owner in self.column(me) + self.column(self.y_peer):
            self.copy(self.held(part, owner), part, owner, self.across, self.c_peer).wait_send()


def relay_sems(parts, count):
    return [pltpu.SemaphoreType.DMA((parts, count)) for _ in range(5)]


def gather_kernel(
    count, stream_any, gain_ref, rows_any, xall, wcol, stream_ref, rows_ref, x_ref, w_ref,
    up, down, over, across, landed, send_w, recv_w, twin_w, own_sem,
):
    me = lax.axis_index("tm")
    call = lax.axis_index("call")
    twin = {"call": 1 - call, "tm": me}
    relay = Relay(count, xall, (up, down, over, across, landed))
    get_stream = pltpu.make_async_copy(stream_any, stream_ref, own_sem.at[0])
    get_rows = pltpu.make_async_copy(rows_any, rows_ref, own_sem.at[1])
    get_stream.start()
    get_rows.start()
    barrier = pltpu.get_barrier_semaphore()
    places = [{"tm": (me + step) % count} for step in range(1, count)] + [twin]
    for where in places:
        pl.semaphore_signal(barrier, inc=1, device_id=where, device_id_type=MESH)
    get_stream.wait()
    x_ref[...] = layer_norm(stream_ref[...], gain_ref[...]).astype(jnp.bfloat16)
    get_rows.wait()
    width = rows_ref.shape[1] // 3
    for head in range(count):
        for part in range(3):
            start = part * width + head * HEAD_DIM
            w_ref[head, :, part * HEAD_DIM : (part + 1) * HEAD_DIM] = rows_ref[
                :, start : start + HEAD_DIM
            ]
    own_x = pltpu.make_async_copy(x_ref, xall.at[0, me], own_sem.at[2])
    own_w = pltpu.make_async_copy(w_ref.at[me], wcol.at[me], own_sem.at[3])
    own_x.start()
    own_w.start()
    pl.semaphore_wait(barrier, len(places))
    relay.start(x_ref, 0)

    def slice_to(place):
        return remote(
            w_ref.at[place], wcol.at[me], send_w.at[place], recv_w.at[me], {"tm": place}
        )

    def slice_on(owner):
        return remote(wcol.at[owner], wcol.at[owner], twin_w.at[owner], recv_w.at[owner], twin)

    @pl.when(me % 2 == call)
    def _():
        for step in range(1, count):
            slice_to((me + step) % count).start()

    relay.start_across(x_ref, 0)
    steps = count // 4 - 1
    relay.step(0, 0)
    relay.step_over(-1, 0)
    for pair in range(count // 2):
        owner = 2 * pair + call

        @pl.when(owner != me)
        def _():
            slice_on(owner).wait_recv()
            slice_on(owner).start()

    for at in range(1, steps):
        relay.step(at, 0)
        relay.step_over(at - 1, 0)
    relay.step_over(steps - 1, 0)
    for pair in range(count // 2):
        owner, other = 2 * pair + call, 2 * pair + 1 - call

        @pl.when(other != me)
        def _():
            slice_on(other).wait_recv()

        @pl.when(owner != me)
        def _():
            slice_on(owner).wait_send()

    @pl.when(me % 2 == call)
    def _():
        for step in range(1, count):
            slice_to((me + step) % count).wait_send()

    relay.receive_across(0)
    relay.finish_sends(0)
    own_x.wait()
    own_w.wait()


def gather_call(stream, gain, w_rows):
    count = lax.axis_size("tm")
    depth = w_rows.shape[0]
    heads = (count, depth, 3 * HEAD_DIM)
    anywhere = pl.BlockSpec(memory_space=pl.ANY)
    vmem = pl.BlockSpec(memory_space=pltpu.VMEM)
    sems = pltpu.SemaphoreType.DMA
    return pl.pallas_call(
        functools.partial(gather_kernel, count),
        out_shape=(
            jax.ShapeDtypeStruct((1, count) + stream.shape, jnp.bfloat16),
            jax.ShapeDtypeStruct(heads, jnp.bfloat16),
        ),
        in_specs=[anywhere, vmem, anywhere],
        out_specs=(anywhere, anywhere),
        scratch_shapes=[
            pltpu.VMEM(stream.shape, jnp.bfloat16),
            pltpu.VMEM(w_rows.shape, jnp.bfloat16),
            pltpu.VMEM(stream.shape, jnp.bfloat16),
            pltpu.VMEM(heads, jnp.bfloat16),
        ]
        + relay_sems(1, count)
        + [sems((count,)), sems((count,)), sems((count,)), sems((4,))],
        compiler_params=pltpu.CompilerParams(
            collective_id=0, has_side_effects=True, vmem_limit_bytes=24 * 1024 * 1024
        ),
        name="gather_frames",
    )(stream, gain, w_rows)


def attend_kernel(
    count, scale, length_ref, q_ref, k_ref, v_ref, out_any, pw1_any, out_ref, wall,
    rows_ref, mixed_ref, landed, send_c, recv_c,
    up, down, over, across, landed_w, twin_w, own_sem,
):
    me = lax.axis_index("tm")
    call = lax.axis_index("call")
    twin = {"call": 1 - call, "tm": me}
    relay = Relay(count, wall, (up, down, over, across, landed_w))
    columns = rows_ref.shape[2]
    sources = (
        out_any,
        pw1_any.at[:, pl.ds(0, columns)],
        pw1_any.at[:, pl.ds(columns, columns)],
    )
    gets = [
        pltpu.make_async_copy(source, rows_ref.at[part], own_sem.at[part])
        for part, source in enumerate(sources)
    ]
    for get in gets:
        get.start()
    greet([{"tm": (me + step) % count} for step in range(1, count)] + [twin])
    for get in gets:
        get.wait()

    def twin_copy(part, owner):
        return remote(
            wall.at[part, owner], wall.at[part, owner], twin_w.at[owner],
            landed_w.at[part, owner], twin,
        )

    def to_twin(part, owner):
        twin_copy(part, owner).start()

    width = LEFT + SPAN
    length = length_ref[call]

    def attend(block):
        first = pl.multiple_of(block * SPAN, SPAN)
        scores = lax.dot_general(
            q_ref[pl.ds(first, SPAN), :],
            k_ref[pl.ds(first, width), :],
            (((1,), (1,)), ((), ())),
            preferred_element_type=jnp.float32,
        )
        key_pos = block * SPAN - LEFT + lax.broadcasted_iota(jnp.int32, (SPAN, width), 1)
        query_pos = block * SPAN + lax.broadcasted_iota(jnp.int32, (SPAN, width), 0)
        allowed = (key_pos >= 0) & ((key_pos < length) | (key_pos == query_pos))
        raised = jnp.where(allowed, jnp.exp(scores * scale), 0.0)
        probs = (raised / jnp.sum(raised, axis=-1, keepdims=True)).astype(jnp.bfloat16)
        mixed = jnp.dot(probs, v_ref[pl.ds(first, width), :], preferred_element_type=jnp.float32)
        return mixed.astype(jnp.bfloat16)

    def attend_and_send(step, carry):
        place = (me + step) % count
        mixed_ref[place] = attend(place)
        remote(
            mixed_ref.at[place], landed.at[me], send_c.at[place], recv_c.at[me], {"tm": place}
        ).start()
        return carry

    own = pltpu.make_async_copy(rows_ref, wall.at[:, me], own_sem.at[3])
    own.start()
    for part in (call, 2):
        relay.start(rows_ref.at[part], part)
    for part in range(3):
        relay.start_across(rows_ref.at[part], part)
    steps = count // 4 - 1

    def relay_step(at):
        relay.step(at, call, to_twin)
        relay.step(at, 2)
        relay.step_over(at - 1, call, to_twin)
        relay.step_over(at - 1, 2)

    lax.fori_loop(1, count // 2, attend_and_send, 0)
    relay_step(0)
    lax.fori_loop(count // 2, count, attend_and_send, 0)
    landed[me] = attend(me)
    for at in range(1, steps):
        relay_step(at)
    relay.step_over(steps - 1, call, to_twin)
    relay.step_over(steps - 1, 2)
    received = relay.column(me)[1:] + relay.column(relay.y_peer)
    for owner in received:
        relay.pass_across(1 - call, owner)
    for step in range(1, count):
        owner = (me + step) % count
        remote(
            mixed_ref.at[owner], landed.at[owner], send_c.at[owner], recv_c.at[owner],
            {"tm": owner},
        ).wait()
    for pair in range(0, count, 2):
        out_ref[:, pair * HEAD_DIM : (pair + 2) * HEAD_DIM] = jnp.concatenate(
            [landed[pair], landed[pair + 1]], axis=1
        )
    own.wait()
    for part in range(3):
        relay.receive_across(part)
    for owner in received:
        twin_copy(call, owner).wait_send()
    relay.finish_sends(call)
    relay.finish_sends(2)
    for owner in relay.column(me) + relay.column(relay.y_peer):
        relay.copy(wall.at[1 - call, owner], 1 - call, owner, across, relay.c_peer).wait_send()


def attend_call(lengths, queries, keys, values, w_out, w_pw1):
    frames, width = queries.shape
    count = frames // SPAN
    anywhere = pl.BlockSpec(memory_space=pl.ANY)
    vmem = pl.BlockSpec(memory_space=pltpu.VMEM)
    sems = pltpu.SemaphoreType.DMA
    parts, (depth, columns) = 3, w_out.shape
    return pl.pallas_call(
        functools.partial(attend_kernel, count, HEAD_DIM**-0.5),
        out_shape=(
            jax.ShapeDtypeStruct((SPAN, count * width), jnp.bfloat16),
            jax.ShapeDtypeStruct((parts, count, depth, columns), jnp.bfloat16),
        ),
        in_specs=[pl.BlockSpec(memory_space=pltpu.SMEM), vmem, vmem, vmem, anywhere, anywhere],
        out_specs=(vmem, anywhere),
        scratch_shapes=[
            pltpu.VMEM((parts, depth, columns), jnp.bfloat16),
            pltpu.VMEM((count, SPAN, width), jnp.bfloat16),
            pltpu.VMEM((count, SPAN, width), jnp.bfloat16),
            sems((count,)), sems((count,)),
        ]
        + relay_sems(parts, count)
        + [sems((count,)), sems((4,))],
        compiler_params=pltpu.CompilerParams(
            collective_id=1, has_side_effects=True, vmem_limit_bytes=32 * 1024 * 1024
        ),
        name="attend_exchange",
    )(lengths, queries, keys, values, w_out, w_pw1)


def project_kernel(length_ref, context_ref, stream_ref, w_ref, gain_ref, attended_ref, gated_ref):
    rows = stream_ref.shape[0]
    first = lax.axis_index("tm") * rows
    length = length_ref[lax.axis_index("call")]
    valid = first + lax.broadcasted_iota(jnp.int32, (rows, 1), 0) < length
    wide = stream_ref[...].astype(jnp.float32) + contract_with(context_ref[...], w_ref[0])
    attended = jnp.where(valid, wide, 0.0).astype(jnp.bfloat16)
    attended_ref[...] = attended
    conv_in = layer_norm(attended, gain_ref[...]).astype(jnp.bfloat16)
    gated = contract_with(conv_in, w_ref[1]) * jax.nn.sigmoid(contract_with(conv_in, w_ref[2]))
    gated_ref[...] = jnp.where(valid, gated, 0.0).astype(jnp.bfloat16)


def project_call(lengths, context, stream, weights, gain):
    vmem = pl.BlockSpec(memory_space=pltpu.VMEM)
    return pl.pallas_call(
        project_kernel,
        out_shape=(jax.ShapeDtypeStruct(stream.shape, jnp.bfloat16),) * 2,
        in_specs=[pl.BlockSpec(memory_space=pltpu.SMEM)] + [vmem] * 4,
        out_specs=(vmem, vmem),
        compiler_params=pltpu.CompilerParams(vmem_limit_bytes=32 * 1024 * 1024),
        name="project_gate",
    )(lengths, context, stream, weights, gain)


EDGE = 16
STRIP = 128


def conv_kernel(
    count, length_ref, g_ref, taps_ref, gain_ref, bias_ref, out_ref,
    low, high, padded, depth, mine, plane, near, far,
    halo_send, halo_recv, near_send, near_recv, far_send, far_recv,
):
    me = lax.axis_index("tm")
    call = lax.axis_index("call")
    rows, width = depth.shape
    right, left = (me + 1) % count, (me + count - 1) % count
    peers = []
    for flips in range(1, 8):
        spot, side = me, call
        if flips & 1:
            spot = spot + 1 - 2 * (me % 2)
        if flips & 2:
            spot = spot + 2 - 4 * ((me // 2) % 2)
        if flips & 4:
            side = 1 - call
        peers.append({"call": side, "tm": spot})
    hops = [{"tm": (me + hop) % count} for hop in range(4, count, 4)]
    greet([{"tm": right}, {"tm": left}] + peers + hops)
    to_right = remote(
        g_ref.at[pl.ds(rows - EDGE, EDGE)], low, halo_send.at[0], halo_recv.at[0], {"tm": right}
    )
    to_left = remote(
        g_ref.at[pl.ds(0, EDGE)], high, halo_send.at[1], halo_recv.at[1], {"tm": left}
    )
    to_right.start()
    to_left.start()
    padded[EDGE : EDGE + rows, :] = g_ref[...].astype(jnp.float32)
    to_right.wait_recv()
    to_left.wait_recv()
    has_low = jnp.where(me > 0, 1.0, 0.0).astype(jnp.float32)
    has_high = jnp.where(me < count - 1, 1.0, 0.0).astype(jnp.float32)
    padded[0:EDGE, :] = low[...].astype(jnp.float32) * has_low
    padded[EDGE + rows : 2 * EDGE + rows, :] = high[...].astype(jnp.float32) * has_high
    first = me * rows + lax.broadcasted_iota(jnp.int32, (rows, 1), 0)
    valid = jnp.where(first < length_ref[call], 1.0, 0.0).astype(jnp.float32)
    for at in range(0, width, STRIP):
        strip = slice(at, at + STRIP)
        total = jnp.zeros((rows, STRIP), jnp.float32)
        for tap in range(KERNEL):
            start = EDGE - KERNEL // 2 + tap
            total = total + padded[start : start + rows, strip] * taps_ref[tap : tap + 1, strip]
        depth[:, strip] = total
        masked = total * valid
        mine[0:1, strip] = jnp.sum(masked, axis=0, keepdims=True)
        mine[1:2, strip] = jnp.sum(masked * total, axis=0, keepdims=True)
    near_copies = []
    for slot, where in enumerate(peers):
        copy = remote(mine, near.at[slot], near_send.at[slot], near_recv.at[slot], where)
        copy.start()
        near_copies.append(copy)
    for copy in near_copies:
        copy.wait_recv()
    both = mine[...]
    for slot in range(len(peers)):
        both = both + near[slot]
    plane[...] = both
    far_copies = []
    for slot, where in enumerate(hops):
        copy = remote(plane, far.at[slot], far_send.at[slot], far_recv.at[slot], where)
        copy.start()
        far_copies.append(copy)
    for copy in far_copies:
        copy.wait_recv()
    for slot in range(len(hops)):
        both = both + far[slot]
    both = both / (length_ref[0] + length_ref[1]).astype(jnp.float32)
    average = both[0:1]
    spread = lax.rsqrt(both[1:2] - average * average + 1e-05)
    for at in range(0, width, STRIP):
        strip = slice(at, at + STRIP)
        act = (depth[:, strip] - average[:, strip]) * spread[:, strip]
        act = act * gain_ref[:, strip] + bias_ref[:, strip]
        act = act * jax.nn.sigmoid(act)
        out_ref[:, strip] = jnp.where(valid > 0.0, act, 0.0).astype(out_ref.dtype)
    for copy in [to_right, to_left] + near_copies + far_copies:
        copy.wait_send()


def conv_call(count, lengths, gated, taps, gain, bias):
    rows, width = gated.shape
    vmem = pl.BlockSpec(memory_space=pltpu.VMEM)
    sems = pltpu.SemaphoreType.DMA
    far_count = count // 4 - 1
    return pl.pallas_call(
        functools.partial(conv_kernel, count),
        out_shape=jax.ShapeDtypeStruct(gated.shape, jnp.bfloat16),
        in_specs=[pl.BlockSpec(memory_space=pltpu.SMEM)] + [vmem] * 4,
        out_specs=vmem,
        scratch_shapes=[
            pltpu.VMEM((EDGE, width), jnp.bfloat16),
            pltpu.VMEM((EDGE, width), jnp.bfloat16),
            pltpu.VMEM((rows + 2 * EDGE, width), jnp.float32),
            pltpu.VMEM((rows, width), jnp.float32),
            pltpu.VMEM((2, width), jnp.float32),
            pltpu.VMEM((2, width), jnp.float32),
            pltpu.VMEM((7, 2, width), jnp.float32),
            pltpu.VMEM((far_count, 2, width), jnp.float32),
            sems((2,)), sems((2,)), sems((7,)), sems((7,)), sems((far_count,)), sems((far_count,)),
        ],
        compiler_params=pltpu.CompilerParams(
            collective_id=2, has_side_effects=True, vmem_limit_bytes=32 * 1024 * 1024
        ),
        name="conv_norm",
    )(lengths, gated, taps, gain, bias)


def one_head_each(
    frames, lengths, ln_attn_gain, w_qkv, w_out, ln_conv_gain, w_pw1, dw_kernel, bn_gain, bn_bias
):
    stream = frames[0]
    model_width = stream.shape[1]
    count = lax.axis_size("tm")
    all_frames, w_columns = gather_call(stream, ln_attn_gain[None], w_qkv)
    packed = contract_with(
        all_frames.reshape(-1, model_width), w_columns.reshape(model_width, -1)
    ).astype(jnp.bfloat16)
    queries = packed[:, :HEAD_DIM]
    keys = jnp.pad(packed[:, HEAD_DIM : 2 * HEAD_DIM], ((LEFT, 0), (0, 0)))
    values = jnp.pad(packed[:, 2 * HEAD_DIM :], ((LEFT, 0), (0, 0)))
    context, weights = attend_call(lengths, queries, keys, values, w_out, w_pw1)
    weights = weights.reshape(3, model_width, model_width)
    attended, gated = project_call(lengths, context, stream, weights, ln_conv_gain[None])
    conv_act = conv_call(count, lengths, gated, dw_kernel, bn_gain[None], bn_bias[None])
    return (attended[None], conv_act[None])


def fits_one_head(mesh):
    return mesh.shape["tm"] == 16 and mesh.shape["call"] == 2


def solution(mesh):
    return jax.shard_map(
        one_head_each if fits_one_head(mesh) else on_device,
        mesh=mesh,
        in_specs=(
            P("call", "tm", None),
            P(),
            P(),
            P("tm", None),
            P("tm", None),
            P(),
            P("tm", None),
            P(),
            P(),
            P(),
        ),
        out_specs=(P("call", "tm", None), P("call", "tm", None)),
        check_vma=False,
    )
```

```python
import functools

import jax
import jax.numpy as jnp
from jax import lax
from jax.experimental import pallas as pl
from jax.experimental.pallas import tpu as pltpu
from jax.sharding import PartitionSpec as P

HEAD_DIM = 64
SPAN = 128
LEFT = 1024
KERNEL = 9


def passed_along(value, axis, steps):
    count = lax.axis_size(axis)
    first, last = (max(0, -steps), min(count, count - steps))
    return lax.ppermute(value, axis, [(source, source + steps) for source in range(first, last)])


def with_halo(cells, sides, width):
    for axis, dim in sides:
        count = lax.axis_size(axis)
        ends = count - 1
        head = lax.slice_in_dim(cells, 0, width, axis=dim)
        tail = lax.slice_in_dim(cells, cells.shape[dim] - width, cells.shape[dim], axis=dim)
        cells = jnp.concatenate(
            [
                lax.ppermute(tail, axis, [(i, (i + 1) % count) for i in range(ends)]),
                cells,
                lax.ppermute(head, axis, [((i + 1) % count, i) for i in range(ends)]),
            ],
            axis=dim,
        )
    return cells


def layer_norm(values, gain_vec):
    wide = values.astype(jnp.float32)
    center = wide - jnp.mean(wide, axis=-1, keepdims=True)
    spread = jnp.mean(center * center, axis=-1, keepdims=True)
    return center * lax.rsqrt(spread + 1e-05) * gain_vec


def contract_with(left, rows_piece):
    return jnp.dot(left, rows_piece, preferred_element_type=jnp.float32)


def on_device(
    frames, lengths, ln_attn_gain, w_qkv, w_out, ln_conv_gain, w_pw1, dw_kernel, bn_gain, bn_bias
):
    stream = frames[0]
    frame_count, model_width = stream.shape
    head_count = model_width // HEAD_DIM
    length = lax.dynamic_index_in_dim(lengths, lax.axis_index("call"), 0, keepdims=False)
    first_row = lax.axis_index("tm") * frame_count
    query_pos = first_row + jnp.arange(frame_count, dtype=jnp.int32)
    frame_valid = query_pos < length
    normed = layer_norm(stream, ln_attn_gain).astype(jnp.bfloat16)
    prior_blocks = LEFT // frame_count
    packed = contract_with(normed, lax.all_gather(w_qkv, "tm", axis=0, tiled=True))
    queries = packed[:, :model_width].astype(jnp.bfloat16)
    key_value = jnp.stack(
        [
            packed[:, model_width : 2 * model_width].astype(jnp.bfloat16),
            packed[:, 2 * model_width :].astype(jnp.bfloat16),
        ]
    )
    blocks = []
    current = key_value
    for hop_index in range(prior_blocks):
        current = passed_along(current, "tm", 1)
        blocks.append(current)
    context_kv = jnp.concatenate(blocks[::-1] + [key_value], axis=1)
    key_count = context_kv.shape[1]
    key_pos = first_row - prior_blocks * frame_count + jnp.arange(key_count, dtype=jnp.int32)
    span_first = query_pos // SPAN * SPAN
    allowed = (key_pos[None, :] >= 0) & (key_pos[None, :] >= span_first[:, None] - LEFT)
    allowed = allowed & (key_pos[None, :] < span_first[:, None] + SPAN)
    allowed = allowed & ((key_pos[None, :] < length) | (key_pos[None, :] == query_pos[:, None]))
    group_size = 4
    group_count = head_count // group_size
    query_groups = queries.reshape(frame_count, group_count, group_size, HEAD_DIM).transpose(
        1, 0, 2, 3
    )
    key_groups = (
        context_kv[0].reshape(key_count, group_count, group_size, HEAD_DIM).transpose(1, 0, 2, 3)
    )
    value_groups = (
        context_kv[1].reshape(key_count, group_count, group_size, HEAD_DIM).transpose(1, 0, 2, 3)
    )
    scale_factor = 1.0 / jnp.sqrt(jnp.float32(HEAD_DIM))

    def attend_group(operands):
        query_part, key_part, value_part = operands
        scores = (
            jnp.einsum("qhd,khd->hqk", query_part, key_part, preferred_element_type=jnp.float32)
            * scale_factor
        )
        raised = jnp.where(allowed[None], jnp.exp(scores), 0.0)
        probs = (raised / jnp.sum(raised, axis=-1, keepdims=True)).astype(jnp.bfloat16)
        mixed = jnp.einsum("hqk,khd->qhd", probs, value_part, preferred_element_type=jnp.float32)
        return mixed.astype(jnp.bfloat16)

    context = lax.map(attend_group, (query_groups, key_groups, value_groups))
    context = context.transpose(1, 0, 2, 3).reshape(frame_count, model_width)
    projected = contract_with(context, lax.all_gather(w_out, "tm", axis=0, tiled=True))
    attended = jnp.where(frame_valid[:, None], stream.astype(jnp.float32) + projected, 0.0).astype(
        jnp.bfloat16
    )
    conv_in = layer_norm(attended, ln_conv_gain).astype(jnp.bfloat16)
    expanded = contract_with(conv_in, lax.all_gather(w_pw1, "tm", axis=0, tiled=True))
    gated = expanded[:, :model_width] * jax.nn.sigmoid(expanded[:, model_width:])
    gated = jnp.where(frame_valid[:, None], gated, 0.0).astype(jnp.bfloat16)
    padded = with_halo(gated, (("tm", 0),), KERNEL // 2)
    depthwise = jnp.zeros((frame_count, model_width), jnp.float32)
    for tap_index in range(KERNEL):
        depthwise = (
            depthwise
            + padded[tap_index : tap_index + frame_count].astype(jnp.float32) * dw_kernel[tap_index]
        )
    masked = jnp.where(frame_valid[:, None], depthwise, 0.0)
    first_moment, second_moment = lax.psum(
        (jnp.sum(masked, axis=0), jnp.sum(masked * depthwise, axis=0)), ("call", "tm")
    )
    count_all = jnp.sum(lengths).astype(jnp.float32)
    average = first_moment / count_all
    second = second_moment / count_all
    normal_act = (depthwise - average) * lax.rsqrt(
        second - average * average + 1e-05
    ) * bn_gain + bn_bias
    activated = normal_act * jax.nn.sigmoid(normal_act)
    conv_act = jnp.where(frame_valid[:, None], activated, 0.0).astype(jnp.bfloat16)
    return (attended[None], conv_act[None])


MESH = pl.DeviceIdType.MESH


def remote(source, target, send_sem, recv_sem, where):
    return pltpu.make_async_remote_copy(
        src_ref=source,
        dst_ref=target,
        send_sem=send_sem,
        recv_sem=recv_sem,
        device_id=where,
        device_id_type=MESH,
    )


EDGE = 16
STRIP = 128


class Relay:
    def __init__(self, count, buffer, sems):
        self.count = count
        self.buffer = buffer
        self.up, self.down, self.over, self.across, self.landed = sems
        self.me = lax.axis_index("tm")
        self.planes = count // 4
        self.plane = self.me // 4
        self.y_peer = self.me + 2 - 4 * ((self.me // 2) % 2)
        self.c_peer = self.me + 1 - 2 * (self.me % 2)

    def copy(self, source, part, owner, send, place):
        return remote(
            source,
            self.buffer.at[part, owner],
            send.at[part, owner],
            self.landed.at[part, owner],
            {"tm": place % self.count},
        )

    def held(self, part, owner):
        return self.buffer.at[part, owner]

    def arrived(self, part, owner):
        self.copy(self.held(part, owner), part, owner, self.across, self.c_peer).wait_recv()

    def start(self, source, part):
        me = self.me

        @pl.when(self.plane < self.planes - 1)
        def _():
            self.copy(source, part, me, self.up, me + 4).start()

        @pl.when(self.plane > 0)
        def _():
            self.copy(source, part, me, self.down, me + self.count - 4).start()

        self.copy(source, part, me, self.over, self.y_peer).start()

    def start_across(self, source, part):
        self.copy(source, part, self.me, self.across, self.c_peer).start()

    def step(self, at, part, extra=None):
        me = self.me
        far = 4 * (at + 1)

        @pl.when(self.plane > at)
        def _():
            owner = me - far
            self.arrived(part, owner)
            held = self.held(part, owner)

            @pl.when(self.plane < self.planes - 1)
            def _():
                self.copy(held, part, owner, self.up, me + 4).start()

            self.copy(held, part, owner, self.over, self.y_peer).start()
            if extra is not None:
                extra(part, owner)
            self.copy(held, part, owner, self.across, self.c_peer).start()

        @pl.when(self.plane + at + 1 < self.planes)
        def _():
            owner = me + far
            self.arrived(part, owner)
            held = self.held(part, owner)

            @pl.when(self.plane > 0)
            def _():
                self.copy(held, part, owner, self.down, me + self.count - 4).start()

            self.copy(held, part, owner, self.over, self.y_peer).start()
            if extra is not None:
                extra(part, owner)
            self.copy(held, part, owner, self.across, self.c_peer).start()

    def pass_across(self, part, owner, extra=None):
        self.arrived(part, owner)
        if extra is not None:
            extra(part, owner)
        self.copy(self.held(part, owner), part, owner, self.across, self.c_peer).start()

    def step_over(self, at, part, extra=None):
        if at < 0:
            self.pass_across(part, self.y_peer, extra)
            return
        far = 4 * (at + 1)

        @pl.when(self.plane > at)
        def _():
            self.pass_across(part, self.y_peer - far, extra)

        @pl.when(self.plane + at + 1 < self.planes)
        def _():
            self.pass_across(part, self.y_peer + far, extra)

    def column(self, base):
        return [(base + hop) % self.count for hop in range(0, self.count, 4)]

    def receive_across(self, part):
        both = self.c_peer + self.y_peer - self.me
        for owner in self.column(self.c_peer) + self.column(both):
            self.arrived(part, owner)

    def finish_sends(self, part):
        me = self.me
        for owner in self.column(me):
            plane = owner // 4

            @pl.when((plane <= self.plane) & (self.plane < self.planes - 1))
            def _():
                self.copy(self.held(part, owner), part, owner, self.up, me + 4).wait_send()

            @pl.when((plane >= self.plane) & (self.plane > 0))
            def _():
                place = me + self.count - 4
                self.copy(self.held(part, owner), part, owner, self.down, place).wait_send()

            self.copy(self.held(part, owner), part, owner, self.over, self.y_peer).wait_send()
        for owner in self.column(me) + self.column(self.y_peer):
            self.copy(self.held(part, owner), part, owner, self.across, self.c_peer).wait_send()


def relay_sems(parts, count):
    return [pltpu.SemaphoreType.DMA((parts, count)) for _ in range(5)]


def layer_kernel(
    count, scale, length_ref, stream_any, gain1_any, rows_any, out_any, gain2_any, pw1_any,
    taps_any, bn_gain_any, bn_bias_any, attended_ref, out_ref,
    stream_ref, gain1_ref, rows_ref, gain2_ref, taps_ref, gain_ref, bias_ref,
    x_ref, w_ref, xall, wcol, q_ref, k_ref, v_ref, parts_ref, wall, mixed_ref, landed,
    context, g_ref, low, high, padded, depth, mine, plane, near, far,
    f_up, f_down, f_over, f_across, f_landed, send_w, recv_w, twin_f,
    up, down, over, across, landed_w, twin_w, send_c, recv_c,
    halo_send, halo_recv, near_send, near_recv, far_send, far_recv, own_sem, get_sem,
):
    me = lax.axis_index("tm")
    call = lax.axis_index("call")
    twin = {"call": 1 - call, "tm": me}
    frames = Relay(count, xall, (f_up, f_down, f_over, f_across, f_landed))
    relay = Relay(count, wall, (up, down, over, across, landed_w))
    columns = parts_ref.shape[2]
    loads = (
        (stream_any, stream_ref),
        (gain1_any, gain1_ref),
        (rows_any, rows_ref),
        (out_any, parts_ref.at[0]),
        (pw1_any.at[:, pl.ds(0, columns)], parts_ref.at[1]),
        (pw1_any.at[:, pl.ds(columns, columns)], parts_ref.at[2]),
        (gain2_any, gain2_ref),
        (taps_any, taps_ref),
        (bn_gain_any, gain_ref),
        (bn_bias_any, bias_ref),
    )
    gets = [
        pltpu.make_async_copy(source, target, get_sem.at[at])
        for at, (source, target) in enumerate(loads)
    ]
    for get in gets:
        get.start()
    peers = []
    for flips in range(1, 8):
        spot, side = me, call
        if flips & 1:
            spot = spot + 1 - 2 * (me % 2)
        if flips & 2:
            spot = spot + 2 - 4 * ((me // 2) % 2)
        if flips & 4:
            side = 1 - call
        peers.append({"call": side, "tm": spot})
    hops = [{"tm": (me + hop) % count} for hop in range(4, count, 4)]
    barrier = pltpu.get_barrier_semaphore()
    places = [{"tm": (me + step) % count} for step in range(1, count)]
    places = places + [where for at, where in enumerate(peers) if at >= 3]
    for where in places:
        pl.semaphore_signal(barrier, inc=1, device_id=where, device_id_type=MESH)
    k_ref[0:LEFT, :] = jnp.zeros((LEFT, HEAD_DIM), jnp.bfloat16)
    v_ref[0:LEFT, :] = jnp.zeros((LEFT, HEAD_DIM), jnp.bfloat16)
    for get in gets:
        get.wait()
    x_ref[...] = layer_norm(stream_ref[...], gain1_ref[...]).astype(jnp.bfloat16)
    width = rows_ref.shape[1] // 3
    for head in range(count):
        for part in range(3):
            start = part * width + head * HEAD_DIM
            w_ref[head, :, part * HEAD_DIM : (part + 1) * HEAD_DIM] = rows_ref[
                :, start : start + HEAD_DIM
            ]
    own_x = pltpu.make_async_copy(x_ref, xall.at[0, me], own_sem.at[0])
    own_w = pltpu.make_async_copy(w_ref.at[me], wcol.at[me], own_sem.at[1])
    own_x.start()
    own_w.start()
    pl.semaphore_wait(barrier, len(places))
    frames.start(x_ref, 0)

    def slice_to(place):
        return remote(
            w_ref.at[place], wcol.at[me], send_w.at[place], recv_w.at[me], {"tm": place}
        )

    def slice_on(owner):
        return remote(wcol.at[owner], wcol.at[owner], twin_f.at[owner], recv_w.at[owner], twin)

    @pl.when(me % 2 == call)
    def _():
        for step in range(1, count):
            slice_to((me + step) % count).start()

    frames.start_across(x_ref, 0)
    steps = count // 4 - 1
    frames.step(0, 0)
    frames.step_over(-1, 0)
    for pair in range(count // 2):
        owner = 2 * pair + call

        @pl.when(owner != me)
        def _():
            slice_on(owner).wait_recv()
            slice_on(owner).start()

    for at in range(1, steps):
        frames.step(at, 0)
        frames.step_over(at - 1, 0)
    frames.step_over(steps - 1, 0)
    own = pltpu.make_async_copy(parts_ref, wall.at[:, me], own_sem.at[2])
    own.start()
    for part in (call, 2):
        relay.start(parts_ref.at[part], part)
    for part in range(3):
        relay.start_across(parts_ref.at[part], part)
    for pair in range(count // 2):
        owner, other = 2 * pair + call, 2 * pair + 1 - call

        @pl.when(other != me)
        def _():
            slice_on(other).wait_recv()

        @pl.when(owner != me)
        def _():
            slice_on(owner).wait_send()

    @pl.when(me % 2 == call)
    def _():
        for step in range(1, count):
            slice_to((me + step) % count).wait_send()

    own_x.wait()
    own_w.wait()
    frames.receive_across(0)
    w_columns = wcol[...].reshape(-1, 3 * HEAD_DIM)

    def project_block(block, carry):
        first = pl.multiple_of(block * SPAN, SPAN)
        packed = contract_with(xall[0, block], w_columns).astype(jnp.bfloat16)
        q_ref[pl.ds(first, SPAN), :] = packed[:, :HEAD_DIM]
        k_ref[pl.ds(first + LEFT, SPAN), :] = packed[:, HEAD_DIM : 2 * HEAD_DIM]
        v_ref[pl.ds(first + LEFT, SPAN), :] = packed[:, 2 * HEAD_DIM :]
        return carry

    lax.fori_loop(0, count, project_block, 0)

    def twin_copy(part, owner):
        return remote(
            wall.at[part, owner], wall.at[part, owner], twin_w.at[owner],
            landed_w.at[part, owner], twin,
        )

    def to_twin(part, owner):
        twin_copy(part, owner).start()

    width = LEFT + SPAN
    length = length_ref[call]

    def attend(block):
        first = pl.multiple_of(block * SPAN, SPAN)
        scores = lax.dot_general(
            q_ref[pl.ds(first, SPAN), :],
            k_ref[pl.ds(first, width), :],
            (((1,), (1,)), ((), ())),
            preferred_element_type=jnp.float32,
        )
        key_pos = block * SPAN - LEFT + lax.broadcasted_iota(jnp.int32, (SPAN, width), 1)
        query_pos = block * SPAN + lax.broadcasted_iota(jnp.int32, (SPAN, width), 0)
        allowed = (key_pos >= 0) & ((key_pos < length) | (key_pos == query_pos))
        raised = jnp.where(allowed, jnp.exp(scores * scale), 0.0)
        probs = (raised / jnp.sum(raised, axis=-1, keepdims=True)).astype(jnp.bfloat16)
        mixed = jnp.dot(probs, v_ref[pl.ds(first, width), :], preferred_element_type=jnp.float32)
        return mixed.astype(jnp.bfloat16)

    def attend_and_send(step, carry):
        place = (me + step) % count
        mixed_ref[place] = attend(place)
        remote(
            mixed_ref.at[place], landed.at[me], send_c.at[place], recv_c.at[me], {"tm": place}
        ).start()
        return carry

    def relay_step(at):
        relay.step(at, call, to_twin)
        relay.step(at, 2)
        relay.step_over(at - 1, call, to_twin)
        relay.step_over(at - 1, 2)

    lax.fori_loop(1, count // 2, attend_and_send, 0)
    relay_step(0)
    lax.fori_loop(count // 2, count, attend_and_send, 0)
    landed[me] = attend(me)
    for at in range(1, steps):
        relay_step(at)
    relay.step_over(steps - 1, call, to_twin)
    relay.step_over(steps - 1, 2)
    received = relay.column(me)[1:] + relay.column(relay.y_peer)
    for owner in received:
        relay.pass_across(1 - call, owner)
    for step in range(1, count):
        owner = (me + step) % count
        remote(
            mixed_ref.at[owner], landed.at[owner], send_c.at[owner], recv_c.at[owner],
            {"tm": owner},
        ).wait()
    for pair in range(0, count, 2):
        context[:, pair * HEAD_DIM : (pair + 2) * HEAD_DIM] = jnp.concatenate(
            [landed[pair], landed[pair + 1]], axis=1
        )
    own.wait()
    for part in range(3):
        relay.receive_across(part)
    rows, width = depth.shape
    valid = me * rows + lax.broadcasted_iota(jnp.int32, (rows, 1), 0) < length
    weights = [wall[part].reshape(width, width) for part in range(3)]
    wide = stream_ref[...].astype(jnp.float32) + contract_with(context[...], weights[0])
    attended = jnp.where(valid, wide, 0.0).astype(jnp.bfloat16)
    attended_ref[...] = attended
    conv_in = layer_norm(attended, gain2_ref[...]).astype(jnp.bfloat16)
    gate = jax.nn.sigmoid(contract_with(conv_in, weights[2]))
    gated = contract_with(conv_in, weights[1]) * gate
    g_ref[...] = jnp.where(valid, gated, 0.0).astype(jnp.bfloat16)
    right, left = (me + 1) % count, (me + count - 1) % count
    to_right = remote(
        g_ref.at[pl.ds(rows - EDGE, EDGE)], low, halo_send.at[0], halo_recv.at[0], {"tm": right}
    )
    to_left = remote(
        g_ref.at[pl.ds(0, EDGE)], high, halo_send.at[1], halo_recv.at[1], {"tm": left}
    )
    to_right.start()
    to_left.start()
    padded[EDGE : EDGE + rows, :] = g_ref[...].astype(jnp.float32)
    to_right.wait_recv()
    to_left.wait_recv()
    has_low = jnp.where(me > 0, 1.0, 0.0).astype(jnp.float32)
    has_high = jnp.where(me < count - 1, 1.0, 0.0).astype(jnp.float32)
    padded[0:EDGE, :] = low[...].astype(jnp.float32) * has_low
    padded[EDGE + rows : 2 * EDGE + rows, :] = high[...].astype(jnp.float32) * has_high
    first = me * rows + lax.broadcasted_iota(jnp.int32, (rows, 1), 0)
    valid = jnp.where(first < length_ref[call], 1.0, 0.0).astype(jnp.float32)
    for at in range(0, width, STRIP):
        strip = slice(at, at + STRIP)
        total = jnp.zeros((rows, STRIP), jnp.float32)
        for tap in range(KERNEL):
            start = EDGE - KERNEL // 2 + tap
            total = total + padded[start : start + rows, strip] * taps_ref[tap : tap + 1, strip]
        depth[:, strip] = total
        masked = total * valid
        mine[0:1, strip] = jnp.sum(masked, axis=0, keepdims=True)
        mine[1:2, strip] = jnp.sum(masked * total, axis=0, keepdims=True)
    near_copies = []
    for slot, where in enumerate(peers):
        copy = remote(mine, near.at[slot], near_send.at[slot], near_recv.at[slot], where)
        copy.start()
        near_copies.append(copy)
    for copy in near_copies:
        copy.wait_recv()
    both = mine[...]
    for slot in range(len(peers)):
        both = both + near[slot]
    plane[...] = both
    far_copies = []
    for slot, where in enumerate(hops):
        copy = remote(plane, far.at[slot], far_send.at[slot], far_recv.at[slot], where)
        copy.start()
        far_copies.append(copy)
    for copy in far_copies:
        copy.wait_recv()
    for slot in range(len(hops)):
        both = both + far[slot]
    both = both / (length_ref[0] + length_ref[1]).astype(jnp.float32)
    average = both[0:1]
    spread = lax.rsqrt(both[1:2] - average * average + 1e-05)
    for at in range(0, width, STRIP):
        strip = slice(at, at + STRIP)
        act = (depth[:, strip] - average[:, strip]) * spread[:, strip]
        act = act * gain_ref[:, strip] + bias_ref[:, strip]
        act = act * jax.nn.sigmoid(act)
        out_ref[:, strip] = jnp.where(valid > 0.0, act, 0.0).astype(out_ref.dtype)
    for copy in [to_right, to_left] + near_copies + far_copies:
        copy.wait_send()


    for owner in received:
        twin_copy(call, owner).wait_send()
    relay.finish_sends(call)
    relay.finish_sends(2)
    for owner in relay.column(me) + relay.column(relay.y_peer):
        relay.copy(wall.at[1 - call, owner], 1 - call, owner, across, relay.c_peer).wait_send()
    frames.finish_sends(0)


def layer_call(lengths, stream, gain1, w_qkv, w_out, gain2, w_pw1, taps, bn_gain, bn_bias):
    rows, width = stream.shape
    count = lax.axis_size("tm")
    wide, deep = jnp.float32, jnp.bfloat16
    depth, planes = w_out.shape[0], count // 4
    total = count * rows
    anywhere = pl.BlockSpec(memory_space=pl.ANY)
    vmem = pl.BlockSpec(memory_space=pltpu.VMEM)
    buffers = [
        (stream.shape, deep), ((1, width), wide), (w_qkv.shape, deep), ((1, width), wide),
        (taps.shape, wide), ((1, width), wide), ((1, width), wide),
        (stream.shape, deep), ((count, depth, 3 * HEAD_DIM), deep),
        ((1, count, rows, width), deep), ((count, depth, 3 * HEAD_DIM), deep),
        ((total, HEAD_DIM), deep), ((total + LEFT, HEAD_DIM), deep),
        ((total + LEFT, HEAD_DIM), deep),
        ((3, depth, width), deep), ((3, count, depth, width), deep),
        ((count, rows, HEAD_DIM), deep), ((count, rows, HEAD_DIM), deep),
        (stream.shape, deep), (stream.shape, deep), ((EDGE, width), deep), ((EDGE, width), deep),
        ((rows + 2 * EDGE, width), wide), ((rows, width), wide), ((2, width), wide),
        ((2, width), wide), ((7, 2, width), wide), ((planes - 1, 2, width), wide),
    ]
    counts = [(count,)] * 3, [(count,)] * 3, [2, 2, 7, 7, planes - 1, planes - 1, 3, 10]
    sems = pltpu.SemaphoreType.DMA
    return pl.pallas_call(
        functools.partial(layer_kernel, count, HEAD_DIM**-0.5),
        out_shape=(jax.ShapeDtypeStruct(stream.shape, deep),) * 2,
        in_specs=[pl.BlockSpec(memory_space=pltpu.SMEM)] + [anywhere] * 9,
        out_specs=(vmem, vmem),
        scratch_shapes=[pltpu.VMEM(shape, kind) for shape, kind in buffers]
        + relay_sems(1, count)
        + [sems(shape) for shape in counts[0]]
        + relay_sems(3, count)
        + [sems(shape) for shape in counts[1]]
        + [sems((size,)) for size in counts[2]],
        compiler_params=pltpu.CompilerParams(
            collective_id=0, has_side_effects=True, vmem_limit_bytes=48 * 1024 * 1024
        ),
        name="layer",
    )(lengths, stream, gain1, w_qkv, w_out, gain2, w_pw1, taps, bn_gain, bn_bias)


def one_head_each(
    frames, lengths, ln_attn_gain, w_qkv, w_out, ln_conv_gain, w_pw1, dw_kernel, bn_gain, bn_bias
):
    attended, conv_act = layer_call(
        lengths, frames[0], ln_attn_gain[None], w_qkv, w_out, ln_conv_gain[None], w_pw1,
        dw_kernel, bn_gain[None], bn_bias[None],
    )
    return (attended[None], conv_act[None])


def fits_one_head(mesh):
    return mesh.shape["tm"] == 16 and mesh.shape["call"] == 2


def solution(mesh):
    return jax.shard_map(
        one_head_each if fits_one_head(mesh) else on_device,
        mesh=mesh,
        in_specs=(
            P("call", "tm", None),
            P(),
            P(),
            P("tm", None),
            P("tm", None),
            P(),
            P("tm", None),
            P(),
            P(),
            P(),
        ),
        out_specs=(P("call", "tm", None), P("call", "tm", None)),
        check_vma=False,
    )
```

```python
import functools

import jax
import jax.numpy as jnp
from jax import lax
from jax.experimental import pallas as pl
from jax.experimental.pallas import tpu as pltpu
from jax.sharding import PartitionSpec as P

HEAD_DIM = 64
SPAN = 128
LEFT = 1024
KERNEL = 9


def passed_along(value, axis, steps):
    count = lax.axis_size(axis)
    first, last = (max(0, -steps), min(count, count - steps))
    return lax.ppermute(value, axis, [(source, source + steps) for source in range(first, last)])


def with_halo(cells, sides, width):
    for axis, dim in sides:
        count = lax.axis_size(axis)
        ends = count - 1
        head = lax.slice_in_dim(cells, 0, width, axis=dim)
        tail = lax.slice_in_dim(cells, cells.shape[dim] - width, cells.shape[dim], axis=dim)
        cells = jnp.concatenate(
            [
                lax.ppermute(tail, axis, [(i, (i + 1) % count) for i in range(ends)]),
                cells,
                lax.ppermute(head, axis, [((i + 1) % count, i) for i in range(ends)]),
            ],
            axis=dim,
        )
    return cells


def layer_norm(values, gain_vec):
    wide = values.astype(jnp.float32)
    center = wide - jnp.mean(wide, axis=-1, keepdims=True)
    spread = jnp.mean(center * center, axis=-1, keepdims=True)
    return center * lax.rsqrt(spread + 1e-05) * gain_vec


def contract_with(left, rows_piece):
    return jnp.dot(left, rows_piece, preferred_element_type=jnp.float32)


def on_device(
    frames, lengths, ln_attn_gain, w_qkv, w_out, ln_conv_gain, w_pw1, dw_kernel, bn_gain, bn_bias
):
    stream = frames[0]
    frame_count, model_width = stream.shape
    head_count = model_width // HEAD_DIM
    length = lax.dynamic_index_in_dim(lengths, lax.axis_index("call"), 0, keepdims=False)
    first_row = lax.axis_index("tm") * frame_count
    query_pos = first_row + jnp.arange(frame_count, dtype=jnp.int32)
    frame_valid = query_pos < length
    normed = layer_norm(stream, ln_attn_gain).astype(jnp.bfloat16)
    prior_blocks = LEFT // frame_count
    packed = contract_with(normed, lax.all_gather(w_qkv, "tm", axis=0, tiled=True))
    queries = packed[:, :model_width].astype(jnp.bfloat16)
    key_value = jnp.stack(
        [
            packed[:, model_width : 2 * model_width].astype(jnp.bfloat16),
            packed[:, 2 * model_width :].astype(jnp.bfloat16),
        ]
    )
    blocks = []
    current = key_value
    for hop_index in range(prior_blocks):
        current = passed_along(current, "tm", 1)
        blocks.append(current)
    context_kv = jnp.concatenate(blocks[::-1] + [key_value], axis=1)
    key_count = context_kv.shape[1]
    key_pos = first_row - prior_blocks * frame_count + jnp.arange(key_count, dtype=jnp.int32)
    span_first = query_pos // SPAN * SPAN
    allowed = (key_pos[None, :] >= 0) & (key_pos[None, :] >= span_first[:, None] - LEFT)
    allowed = allowed & (key_pos[None, :] < span_first[:, None] + SPAN)
    allowed = allowed & ((key_pos[None, :] < length) | (key_pos[None, :] == query_pos[:, None]))
    group_size = 4
    group_count = head_count // group_size
    query_groups = queries.reshape(frame_count, group_count, group_size, HEAD_DIM).transpose(
        1, 0, 2, 3
    )
    key_groups = (
        context_kv[0].reshape(key_count, group_count, group_size, HEAD_DIM).transpose(1, 0, 2, 3)
    )
    value_groups = (
        context_kv[1].reshape(key_count, group_count, group_size, HEAD_DIM).transpose(1, 0, 2, 3)
    )
    scale_factor = 1.0 / jnp.sqrt(jnp.float32(HEAD_DIM))

    def attend_group(operands):
        query_part, key_part, value_part = operands
        scores = (
            jnp.einsum("qhd,khd->hqk", query_part, key_part, preferred_element_type=jnp.float32)
            * scale_factor
        )
        raised = jnp.where(allowed[None], jnp.exp(scores), 0.0)
        probs = (raised / jnp.sum(raised, axis=-1, keepdims=True)).astype(jnp.bfloat16)
        mixed = jnp.einsum("hqk,khd->qhd", probs, value_part, preferred_element_type=jnp.float32)
        return mixed.astype(jnp.bfloat16)

    context = lax.map(attend_group, (query_groups, key_groups, value_groups))
    context = context.transpose(1, 0, 2, 3).reshape(frame_count, model_width)
    projected = contract_with(context, lax.all_gather(w_out, "tm", axis=0, tiled=True))
    attended = jnp.where(frame_valid[:, None], stream.astype(jnp.float32) + projected, 0.0).astype(
        jnp.bfloat16
    )
    conv_in = layer_norm(attended, ln_conv_gain).astype(jnp.bfloat16)
    expanded = contract_with(conv_in, lax.all_gather(w_pw1, "tm", axis=0, tiled=True))
    gated = expanded[:, :model_width] * jax.nn.sigmoid(expanded[:, model_width:])
    gated = jnp.where(frame_valid[:, None], gated, 0.0).astype(jnp.bfloat16)
    padded = with_halo(gated, (("tm", 0),), KERNEL // 2)
    depthwise = jnp.zeros((frame_count, model_width), jnp.float32)
    for tap_index in range(KERNEL):
        depthwise = (
            depthwise
            + padded[tap_index : tap_index + frame_count].astype(jnp.float32) * dw_kernel[tap_index]
        )
    masked = jnp.where(frame_valid[:, None], depthwise, 0.0)
    first_moment, second_moment = lax.psum(
        (jnp.sum(masked, axis=0), jnp.sum(masked * depthwise, axis=0)), ("call", "tm")
    )
    count_all = jnp.sum(lengths).astype(jnp.float32)
    average = first_moment / count_all
    second = second_moment / count_all
    normal_act = (depthwise - average) * lax.rsqrt(
        second - average * average + 1e-05
    ) * bn_gain + bn_bias
    activated = normal_act * jax.nn.sigmoid(normal_act)
    conv_act = jnp.where(frame_valid[:, None], activated, 0.0).astype(jnp.bfloat16)
    return (attended[None], conv_act[None])


MESH = pl.DeviceIdType.MESH


def remote(source, target, send_sem, recv_sem, where):
    return pltpu.make_async_remote_copy(
        src_ref=source,
        dst_ref=target,
        send_sem=send_sem,
        recv_sem=recv_sem,
        device_id=where,
        device_id_type=MESH,
    )


EDGE = 16
STRIP = 128


class Relay:
    def __init__(self, count, slot, sems):
        self.count = count
        self.held = slot
        self.up, self.down, self.over, self.across, self.landed = sems
        self.me = lax.axis_index("tm")
        self.planes = count // 4
        self.plane = self.me // 4
        self.y_peer = self.me + 2 - 4 * ((self.me // 2) % 2)
        self.c_peer = self.me + 1 - 2 * (self.me % 2)

    def copy(self, source, part, owner, send, place):
        return remote(
            source,
            self.held(part, owner),
            send.at[part, owner],
            self.landed.at[part, owner],
            {"tm": place % self.count},
        )

    def arrived(self, part, owner):
        self.copy(self.held(part, owner), part, owner, self.across, self.c_peer).wait_recv()

    def start(self, source, part):
        me = self.me

        @pl.when(self.plane < self.planes - 1)
        def _():
            self.copy(source, part, me, self.up, me + 4).start()

        @pl.when(self.plane > 0)
        def _():
            self.copy(source, part, me, self.down, me + self.count - 4).start()

        self.copy(source, part, me, self.over, self.y_peer).start()

    def start_across(self, source, part):
        self.copy(source, part, self.me, self.across, self.c_peer).start()

    def step(self, at, part, extra=None):
        me = self.me
        far = 4 * (at + 1)

        @pl.when(self.plane > at)
        def _():
            owner = me - far
            self.arrived(part, owner)
            held = self.held(part, owner)

            @pl.when(self.plane < self.planes - 1)
            def _():
                self.copy(held, part, owner, self.up, me + 4).start()

            self.copy(held, part, owner, self.over, self.y_peer).start()
            if extra is not None:
                extra(part, owner)
            self.copy(held, part, owner, self.across, self.c_peer).start()

        @pl.when(self.plane + at + 1 < self.planes)
        def _():
            owner = me + far
            self.arrived(part, owner)
            held = self.held(part, owner)

            @pl.when(self.plane > 0)
            def _():
                self.copy(held, part, owner, self.down, me + self.count - 4).start()

            self.copy(held, part, owner, self.over, self.y_peer).start()
            if extra is not None:
                extra(part, owner)
            self.copy(held, part, owner, self.across, self.c_peer).start()

    def pass_across(self, part, owner, extra=None):
        self.arrived(part, owner)
        if extra is not None:
            extra(part, owner)
        self.copy(self.held(part, owner), part, owner, self.across, self.c_peer).start()

    def step_over(self, at, part, extra=None):
        if at < 0:
            self.pass_across(part, self.y_peer, extra)
            return
        far = 4 * (at + 1)

        @pl.when(self.plane > at)
        def _():
            self.pass_across(part, self.y_peer - far, extra)

        @pl.when(self.plane + at + 1 < self.planes)
        def _():
            self.pass_across(part, self.y_peer + far, extra)

    def column(self, base):
        return [(base + hop) % self.count for hop in range(0, self.count, 4)]

    def receive_across(self, part):
        both = self.c_peer + self.y_peer - self.me
        for owner in self.column(self.c_peer) + self.column(both):
            self.arrived(part, owner)

    def finish_sends(self, part):
        me = self.me
        for owner in self.column(me):
            plane = owner // 4

            @pl.when((plane <= self.plane) & (self.plane < self.planes - 1))
            def _():
                self.copy(self.held(part, owner), part, owner, self.up, me + 4).wait_send()

            @pl.when((plane >= self.plane) & (self.plane > 0))
            def _():
                place = me + self.count - 4
                self.copy(self.held(part, owner), part, owner, self.down, place).wait_send()

            self.copy(self.held(part, owner), part, owner, self.over, self.y_peer).wait_send()
        for owner in self.column(me) + self.column(self.y_peer):
            self.copy(self.held(part, owner), part, owner, self.across, self.c_peer).wait_send()


def relay_sems(parts, count):
    return [pltpu.SemaphoreType.DMA((parts, count)) for _ in range(5)]


def layer_kernel(
    count, scale, length_ref, stream_any, gain1_any, rows_any, out_any, gain2_any, pw1_any,
    taps_any, bn_gain_any, bn_bias_any, attended_ref, out_ref,
    stream_ref, gain1_ref, rows_ref, gain2_ref, taps_ref, gain_ref, bias_ref,
    x_ref, w_ref, xall, wcol, q_ref, k_ref, v_ref, parts_ref, wall, mixed_ref, landed,
    context, g_ref, low, high, padded, depth, mine, plane, near, far,
    f_up, f_down, f_over, f_across, f_landed, send_w, recv_w, twin_f,
    up, down, over, across, landed_w, twin_w, send_c, recv_c,
    halo_send, halo_recv, near_send, near_recv, far_send, far_recv, own_sem, get_sem,
):
    me = lax.axis_index("tm")
    call = lax.axis_index("call")
    twin = {"call": 1 - call, "tm": me}
    frames = Relay(count, lambda part, owner: xall.at[part, owner], (f_up, f_down, f_over, f_across, f_landed))
    columns = stream_ref.shape[1]
    half = parts_ref.shape[0] // 2

    def half_of(part):
        return pl.ds(pl.multiple_of(part * half, half), half)

    def weight_slot(part, owner):
        return wall.at[owner, half_of(part)]

    relay = Relay(count, weight_slot, (up, down, over, across, landed_w))
    loads = (
        (stream_any, stream_ref),
        (gain1_any, gain1_ref),
        (rows_any, rows_ref),
        (out_any, parts_ref.at[:, pl.ds(0, columns)]),
        (pw1_any, parts_ref.at[:, pl.ds(columns, 2 * columns)]),
        (gain2_any, gain2_ref),
        (taps_any, taps_ref),
        (bn_gain_any, gain_ref),
        (bn_bias_any, bias_ref),
    )
    gets = [
        pltpu.make_async_copy(source, target, get_sem.at[at])
        for at, (source, target) in enumerate(loads)
    ]
    for get in gets:
        get.start()
    peers = []
    for flips in range(1, 8):
        spot, side = me, call
        if flips & 1:
            spot = spot + 1 - 2 * (me % 2)
        if flips & 2:
            spot = spot + 2 - 4 * ((me // 2) % 2)
        if flips & 4:
            side = 1 - call
        peers.append({"call": side, "tm": spot})
    hops = [{"tm": (me + hop) % count} for hop in range(4, count, 4)]
    barrier = pltpu.get_barrier_semaphore()
    places = [{"tm": (me + step) % count} for step in range(1, count)]
    places = places + [where for at, where in enumerate(peers) if at >= 3]
    for where in places:
        pl.semaphore_signal(barrier, inc=1, device_id=where, device_id_type=MESH)
    k_ref[0:LEFT, :] = jnp.zeros((LEFT, HEAD_DIM), jnp.bfloat16)
    v_ref[0:LEFT, :] = jnp.zeros((LEFT, HEAD_DIM), jnp.bfloat16)
    gets[0].wait()
    gets[1].wait()
    x_ref[...] = layer_norm(stream_ref[...], gain1_ref[...]).astype(jnp.bfloat16)
    own_x = pltpu.make_async_copy(x_ref, xall.at[0, me], own_sem.at[0])
    own_w = pltpu.make_async_copy(w_ref.at[me], wcol.at[me], own_sem.at[1])
    own_x.start()
    pl.semaphore_wait(barrier, len(places))
    frames.start(x_ref, 0)
    frames.start_across(x_ref, 0)
    for get in gets[2:]:
        get.wait()
    width = rows_ref.shape[1] // 3
    for head in range(count):
        for part in range(3):
            start = part * width + head * HEAD_DIM
            w_ref[head, :, part * HEAD_DIM : (part + 1) * HEAD_DIM] = rows_ref[
                :, start : start + HEAD_DIM
            ]
    own_w.start()

    def slice_to(place):
        return remote(
            w_ref.at[place], wcol.at[me], send_w.at[place], recv_w.at[me], {"tm": place}
        )

    def slice_on(owner):
        return remote(wcol.at[owner], wcol.at[owner], twin_f.at[owner], recv_w.at[owner], twin)

    @pl.when(me % 2 == call)
    def _():
        for step in range(1, count):
            slice_to((me + step) % count).start()

    steps = count // 4 - 1
    frames.step(0, 0)
    frames.step_over(-1, 0)
    for pair in range(count // 2):
        owner = 2 * pair + call

        @pl.when(owner != me)
        def _():
            slice_on(owner).wait_recv()
            slice_on(owner).start()

    for at in range(1, steps):
        frames.step(at, 0)
        frames.step_over(at - 1, 0)
    frames.step_over(steps - 1, 0)
    own = pltpu.make_async_copy(parts_ref, wall.at[me], own_sem.at[2])
    own.start()
    relay.start(parts_ref.at[half_of(call)], call)
    for part in range(2):
        relay.start_across(parts_ref.at[half_of(part)], part)
    for pair in range(count // 2):
        owner, other = 2 * pair + call, 2 * pair + 1 - call

        @pl.when(other != me)
        def _():
            slice_on(other).wait_recv()

        @pl.when(owner != me)
        def _():
            slice_on(owner).wait_send()

    @pl.when(me % 2 == call)
    def _():
        for step in range(1, count):
            slice_to((me + step) % count).wait_send()

    own_x.wait()
    own_w.wait()
    frames.receive_across(0)
    w_columns = wcol[...].reshape(-1, 3 * HEAD_DIM)

    group = 4 * SPAN

    def project_group(at, carry):
        first = pl.multiple_of(at * group, group)
        rows = xall[0, pl.ds(4 * at, 4)].reshape(group, columns)
        packed = contract_with(rows, w_columns).astype(jnp.bfloat16)
        q_ref[pl.ds(first, group), :] = packed[:, :HEAD_DIM]
        k_ref[pl.ds(first + LEFT, group), :] = packed[:, HEAD_DIM : 2 * HEAD_DIM]
        v_ref[pl.ds(first + LEFT, group), :] = packed[:, 2 * HEAD_DIM :]
        return carry

    lax.fori_loop(0, count // 4, project_group, 0)

    def twin_copy(part, owner):
        return remote(
            weight_slot(part, owner), weight_slot(part, owner), twin_w.at[owner], landed_w.at[part, owner], twin
        )

    def to_twin(part, owner):
        twin_copy(part, owner).start()

    width = LEFT + SPAN
    length = length_ref[call]

    def attend(block):
        first = pl.multiple_of(block * SPAN, SPAN)
        scores = lax.dot_general(
            q_ref[pl.ds(first, SPAN), :],
            k_ref[pl.ds(first, width), :],
            (((1,), (1,)), ((), ())),
            preferred_element_type=jnp.float32,
        )
        key_pos = block * SPAN - LEFT + lax.broadcasted_iota(jnp.int32, (SPAN, width), 1)
        query_pos = block * SPAN + lax.broadcasted_iota(jnp.int32, (SPAN, width), 0)
        allowed = (key_pos >= 0) & ((key_pos < length) | (key_pos == query_pos))
        raised = jnp.where(allowed, jnp.exp(scores * scale), 0.0)
        total = jnp.sum(raised, axis=-1, keepdims=True)
        shrink = jnp.where(total > 1.0, 2.0**-32, 1.0).astype(jnp.float32)
        probs = (raised * shrink * (1.0 / (total * shrink))).astype(jnp.bfloat16)
        mixed = jnp.dot(probs, v_ref[pl.ds(first, width), :], preferred_element_type=jnp.float32)
        return mixed.astype(jnp.bfloat16)

    def attend_and_send(step, carry):
        place = (me + step) % count
        mixed_ref[place] = attend(place)
        remote(
            mixed_ref.at[place], landed.at[me], send_c.at[place], recv_c.at[me], {"tm": place}
        ).start()
        return carry

    def relay_step(at):
        relay.step(at, call, to_twin)
        relay.step_over(at - 1, call, to_twin)

    lax.fori_loop(1, count // 2, attend_and_send, 0)
    relay_step(0)
    lax.fori_loop(count // 2, count, attend_and_send, 0)
    landed[me] = attend(me)
    for at in range(1, steps):
        relay_step(at)
    relay.step_over(steps - 1, call, to_twin)
    received = relay.column(me)[1:] + relay.column(relay.y_peer)
    for owner in received:
        relay.pass_across(1 - call, owner)
    for step in range(1, count):
        owner = (me + step) % count
        remote(
            mixed_ref.at[owner], landed.at[owner], send_c.at[owner], recv_c.at[owner],
            {"tm": owner},
        ).wait()
    for pair in range(0, count, 2):
        context[:, pair * HEAD_DIM : (pair + 2) * HEAD_DIM] = jnp.concatenate(
            [landed[pair], landed[pair + 1]], axis=1
        )
    own.wait()
    for part in range(2):
        relay.receive_across(part)
    rows, width = depth.shape
    valid = me * rows + lax.broadcasted_iota(jnp.int32, (rows, 1), 0) < length
    weights = [
        wall[:, :, at : at + width].reshape(width, width) for at in range(0, 3 * width, width)
    ]
    wide = stream_ref[...].astype(jnp.float32) + contract_with(context[...], weights[0])
    attended = jnp.where(valid, wide, 0.0).astype(jnp.bfloat16)
    attended_ref[...] = attended
    conv_in = layer_norm(attended, gain2_ref[...]).astype(jnp.bfloat16)
    gate = jax.nn.sigmoid(contract_with(conv_in, weights[2]))
    gated = contract_with(conv_in, weights[1]) * gate
    g_ref[...] = jnp.where(valid, gated, 0.0).astype(jnp.bfloat16)
    right, left = (me + 1) % count, (me + count - 1) % count
    to_right = remote(
        g_ref.at[pl.ds(rows - EDGE, EDGE)], low, halo_send.at[0], halo_recv.at[0], {"tm": right}
    )
    to_left = remote(
        g_ref.at[pl.ds(0, EDGE)], high, halo_send.at[1], halo_recv.at[1], {"tm": left}
    )
    to_right.start()
    to_left.start()
    padded[EDGE : EDGE + rows, :] = g_ref[...].astype(jnp.float32)
    to_right.wait_recv()
    to_left.wait_recv()
    has_low = jnp.where(me > 0, 1.0, 0.0).astype(jnp.float32)
    has_high = jnp.where(me < count - 1, 1.0, 0.0).astype(jnp.float32)
    padded[0:EDGE, :] = low[...].astype(jnp.float32) * has_low
    padded[EDGE + rows : 2 * EDGE + rows, :] = high[...].astype(jnp.float32) * has_high
    first = me * rows + lax.broadcasted_iota(jnp.int32, (rows, 1), 0)
    valid = jnp.where(first < length_ref[call], 1.0, 0.0).astype(jnp.float32)
    for at in range(0, width, STRIP):
        strip = slice(at, at + STRIP)
        total = jnp.zeros((rows, STRIP), jnp.float32)
        for tap in range(KERNEL):
            start = EDGE - KERNEL // 2 + tap
            total = total + padded[start : start + rows, strip] * taps_ref[tap : tap + 1, strip]
        depth[:, strip] = total
        masked = total * valid
        mine[0:1, strip] = jnp.sum(masked, axis=0, keepdims=True)
        mine[1:2, strip] = jnp.sum(masked * total, axis=0, keepdims=True)
    near_copies = []
    for slot, where in enumerate(peers):
        copy = remote(mine, near.at[slot], near_send.at[slot], near_recv.at[slot], where)
        copy.start()
        near_copies.append(copy)
    for copy in near_copies:
        copy.wait_recv()
    both = mine[...]
    for slot in range(len(peers)):
        both = both + near[slot]
    plane[...] = both
    far_copies = []
    for slot, where in enumerate(hops):
        copy = remote(plane, far.at[slot], far_send.at[slot], far_recv.at[slot], where)
        copy.start()
        far_copies.append(copy)
    for copy in far_copies:
        copy.wait_recv()
    for slot in range(len(hops)):
        both = both + far[slot]
    both = both / (length_ref[0] + length_ref[1]).astype(jnp.float32)
    average = both[0:1]
    spread = lax.rsqrt(both[1:2] - average * average + 1e-05)
    for at in range(0, width, STRIP):
        strip = slice(at, at + STRIP)
        act = (depth[:, strip] - average[:, strip]) * spread[:, strip]
        act = act * gain_ref[:, strip] + bias_ref[:, strip]
        act = act * jax.nn.sigmoid(act)
        out_ref[:, strip] = jnp.where(valid > 0.0, act, 0.0).astype(out_ref.dtype)
    for copy in [to_right, to_left] + near_copies + far_copies:
        copy.wait_send()


    for owner in received:
        twin_copy(call, owner).wait_send()
    relay.finish_sends(call)
    for owner in relay.column(me) + relay.column(relay.y_peer):
        relay.copy(weight_slot(1 - call, owner), 1 - call, owner, across, relay.c_peer).wait_send()
    frames.finish_sends(0)


def layer_call(lengths, stream, gain1, w_qkv, w_out, gain2, w_pw1, taps, bn_gain, bn_bias):
    rows, width = stream.shape
    count = lax.axis_size("tm")
    wide, deep = jnp.float32, jnp.bfloat16
    depth, planes = w_out.shape[0], count // 4
    total = count * rows
    anywhere = pl.BlockSpec(memory_space=pl.ANY)
    vmem = pl.BlockSpec(memory_space=pltpu.VMEM)
    buffers = [
        (stream.shape, deep), ((1, width), wide), (w_qkv.shape, deep), ((1, width), wide),
        (taps.shape, wide), ((1, width), wide), ((1, width), wide),
        (stream.shape, deep), ((count, depth, 3 * HEAD_DIM), deep),
        ((1, count, rows, width), deep), ((count, depth, 3 * HEAD_DIM), deep),
        ((total, HEAD_DIM), deep), ((total + LEFT, HEAD_DIM), deep),
        ((total + LEFT, HEAD_DIM), deep),
        ((depth, 3 * width), deep), ((count, depth, 3 * width), deep),
        ((count, rows, HEAD_DIM), deep), ((count, rows, HEAD_DIM), deep),
        (stream.shape, deep), (stream.shape, deep), ((EDGE, width), deep), ((EDGE, width), deep),
        ((rows + 2 * EDGE, width), wide), ((rows, width), wide), ((2, width), wide),
        ((2, width), wide), ((7, 2, width), wide), ((planes - 1, 2, width), wide),
    ]
    counts = [(count,)] * 3, [(count,)] * 3, [2, 2, 7, 7, planes - 1, planes - 1, 3, 9]
    sems = pltpu.SemaphoreType.DMA
    return pl.pallas_call(
        functools.partial(layer_kernel, count, HEAD_DIM**-0.5),
        out_shape=(jax.ShapeDtypeStruct(stream.shape, deep),) * 2,
        in_specs=[pl.BlockSpec(memory_space=pltpu.SMEM)] + [anywhere] * 9,
        out_specs=(vmem, vmem),
        scratch_shapes=[pltpu.VMEM(shape, kind) for shape, kind in buffers]
        + relay_sems(1, count)
        + [sems(shape) for shape in counts[0]]
        + relay_sems(2, count)
        + [sems(shape) for shape in counts[1]]
        + [sems((size,)) for size in counts[2]],
        compiler_params=pltpu.CompilerParams(
            collective_id=0, has_side_effects=True, vmem_limit_bytes=48 * 1024 * 1024
        ),
        name="layer",
    )(lengths, stream, gain1, w_qkv, w_out, gain2, w_pw1, taps, bn_gain, bn_bias)


def one_head_each(
    frames, lengths, ln_attn_gain, w_qkv, w_out, ln_conv_gain, w_pw1, dw_kernel, bn_gain, bn_bias
):
    attended, conv_act = layer_call(
        lengths, frames[0], ln_attn_gain[None], w_qkv, w_out, ln_conv_gain[None], w_pw1,
        dw_kernel, bn_gain[None], bn_bias[None],
    )
    return (attended[None], conv_act[None])


def fits_one_head(mesh):
    return mesh.shape["tm"] == 16 and mesh.shape["call"] == 2


def solution(mesh):
    return jax.shard_map(
        one_head_each if fits_one_head(mesh) else on_device,
        mesh=mesh,
        in_specs=(
            P("call", "tm", None),
            P(),
            P(),
            P("tm", None),
            P("tm", None),
            P(),
            P("tm", None),
            P(),
            P(),
            P(),
        ),
        out_specs=(P("call", "tm", None), P("call", "tm", None)),
        check_vma=False,
    )
```

```python
import functools

import jax
import jax.numpy as jnp
from jax import lax
from jax.experimental import pallas as pl
from jax.experimental.pallas import tpu as pltpu
from jax.sharding import PartitionSpec as P

HEAD_DIM = 64
SPAN = 128
LEFT = 1024
KERNEL = 9


def passed_along(value, axis, steps):
    count = lax.axis_size(axis)
    first, last = (max(0, -steps), min(count, count - steps))
    return lax.ppermute(value, axis, [(source, source + steps) for source in range(first, last)])


def with_halo(cells, sides, width):
    for axis, dim in sides:
        count = lax.axis_size(axis)
        ends = count - 1
        head = lax.slice_in_dim(cells, 0, width, axis=dim)
        tail = lax.slice_in_dim(cells, cells.shape[dim] - width, cells.shape[dim], axis=dim)
        cells = jnp.concatenate(
            [
                lax.ppermute(tail, axis, [(i, (i + 1) % count) for i in range(ends)]),
                cells,
                lax.ppermute(head, axis, [((i + 1) % count, i) for i in range(ends)]),
            ],
            axis=dim,
        )
    return cells


def layer_norm(values, gain_vec):
    wide = values.astype(jnp.float32)
    center = wide - jnp.mean(wide, axis=-1, keepdims=True)
    spread = jnp.mean(center * center, axis=-1, keepdims=True)
    return center * lax.rsqrt(spread + 1e-05) * gain_vec


def contract_with(left, rows_piece):
    return jnp.dot(left, rows_piece, preferred_element_type=jnp.float32)


def on_device(
    frames, lengths, ln_attn_gain, w_qkv, w_out, ln_conv_gain, w_pw1, dw_kernel, bn_gain, bn_bias
):
    stream = frames[0]
    frame_count, model_width = stream.shape
    head_count = model_width // HEAD_DIM
    length = lax.dynamic_index_in_dim(lengths, lax.axis_index("call"), 0, keepdims=False)
    first_row = lax.axis_index("tm") * frame_count
    query_pos = first_row + jnp.arange(frame_count, dtype=jnp.int32)
    frame_valid = query_pos < length
    normed = layer_norm(stream, ln_attn_gain).astype(jnp.bfloat16)
    prior_blocks = LEFT // frame_count
    packed = contract_with(normed, lax.all_gather(w_qkv, "tm", axis=0, tiled=True))
    queries = packed[:, :model_width].astype(jnp.bfloat16)
    key_value = jnp.stack(
        [
            packed[:, model_width : 2 * model_width].astype(jnp.bfloat16),
            packed[:, 2 * model_width :].astype(jnp.bfloat16),
        ]
    )
    blocks = []
    current = key_value
    for hop_index in range(prior_blocks):
        current = passed_along(current, "tm", 1)
        blocks.append(current)
    context_kv = jnp.concatenate(blocks[::-1] + [key_value], axis=1)
    key_count = context_kv.shape[1]
    key_pos = first_row - prior_blocks * frame_count + jnp.arange(key_count, dtype=jnp.int32)
    span_first = query_pos // SPAN * SPAN
    allowed = (key_pos[None, :] >= 0) & (key_pos[None, :] >= span_first[:, None] - LEFT)
    allowed = allowed & (key_pos[None, :] < span_first[:, None] + SPAN)
    allowed = allowed & ((key_pos[None, :] < length) | (key_pos[None, :] == query_pos[:, None]))
    group_size = 4
    group_count = head_count // group_size
    query_groups = queries.reshape(frame_count, group_count, group_size, HEAD_DIM).transpose(
        1, 0, 2, 3
    )
    key_groups = (
        context_kv[0].reshape(key_count, group_count, group_size, HEAD_DIM).transpose(1, 0, 2, 3)
    )
    value_groups = (
        context_kv[1].reshape(key_count, group_count, group_size, HEAD_DIM).transpose(1, 0, 2, 3)
    )
    scale_factor = 1.0 / jnp.sqrt(jnp.float32(HEAD_DIM))

    def attend_group(operands):
        query_part, key_part, value_part = operands
        scores = (
            jnp.einsum("qhd,khd->hqk", query_part, key_part, preferred_element_type=jnp.float32)
            * scale_factor
        )
        raised = jnp.where(allowed[None], jnp.exp(scores), 0.0)
        probs = (raised / jnp.sum(raised, axis=-1, keepdims=True)).astype(jnp.bfloat16)
        mixed = jnp.einsum("hqk,khd->qhd", probs, value_part, preferred_element_type=jnp.float32)
        return mixed.astype(jnp.bfloat16)

    context = lax.map(attend_group, (query_groups, key_groups, value_groups))
    context = context.transpose(1, 0, 2, 3).reshape(frame_count, model_width)
    projected = contract_with(context, lax.all_gather(w_out, "tm", axis=0, tiled=True))
    attended = jnp.where(frame_valid[:, None], stream.astype(jnp.float32) + projected, 0.0).astype(
        jnp.bfloat16
    )
    conv_in = layer_norm(attended, ln_conv_gain).astype(jnp.bfloat16)
    expanded = contract_with(conv_in, lax.all_gather(w_pw1, "tm", axis=0, tiled=True))
    gated = expanded[:, :model_width] * jax.nn.sigmoid(expanded[:, model_width:])
    gated = jnp.where(frame_valid[:, None], gated, 0.0).astype(jnp.bfloat16)
    padded = with_halo(gated, (("tm", 0),), KERNEL // 2)
    depthwise = jnp.zeros((frame_count, model_width), jnp.float32)
    for tap_index in range(KERNEL):
        depthwise = (
            depthwise
            + padded[tap_index : tap_index + frame_count].astype(jnp.float32) * dw_kernel[tap_index]
        )
    masked = jnp.where(frame_valid[:, None], depthwise, 0.0)
    first_moment, second_moment = lax.psum(
        (jnp.sum(masked, axis=0), jnp.sum(masked * depthwise, axis=0)), ("call", "tm")
    )
    count_all = jnp.sum(lengths).astype(jnp.float32)
    average = first_moment / count_all
    second = second_moment / count_all
    normal_act = (depthwise - average) * lax.rsqrt(
        second - average * average + 1e-05
    ) * bn_gain + bn_bias
    activated = normal_act * jax.nn.sigmoid(normal_act)
    conv_act = jnp.where(frame_valid[:, None], activated, 0.0).astype(jnp.bfloat16)
    return (attended[None], conv_act[None])


MESH = pl.DeviceIdType.MESH


def remote(source, target, send_sem, recv_sem, where):
    return pltpu.make_async_remote_copy(
        src_ref=source,
        dst_ref=target,
        send_sem=send_sem,
        recv_sem=recv_sem,
        device_id=where,
        device_id_type=MESH,
    )


EDGE = 16
STRIP = 128


class Relay:
    def __init__(self, count, buffer, sems):
        self.count = count
        self.buffer = buffer
        self.up, self.down, self.over, self.across, self.landed = sems
        self.me = lax.axis_index("tm")
        self.planes = count // 4
        self.plane = self.me // 4
        self.y_peer = self.me + 2 - 4 * ((self.me // 2) % 2)
        self.c_peer = self.me + 1 - 2 * (self.me % 2)

    def copy(self, source, part, owner, send, place):
        return remote(
            source,
            self.buffer.at[part, owner],
            send.at[part, owner],
            self.landed.at[part, owner],
            {"tm": place % self.count},
        )

    def held(self, part, owner):
        return self.buffer.at[part, owner]

    def arrived(self, part, owner):
        self.copy(self.held(part, owner), part, owner, self.across, self.c_peer).wait_recv()

    def start(self, source, part):
        me = self.me

        @pl.when(self.plane < self.planes - 1)
        def _():
            self.copy(source, part, me, self.up, me + 4).start()

        @pl.when(self.plane > 0)
        def _():
            self.copy(source, part, me, self.down, me + self.count - 4).start()

        self.copy(source, part, me, self.over, self.y_peer).start()

    def start_across(self, source, part):
        self.copy(source, part, self.me, self.across, self.c_peer).start()

    def step(self, at, part, extra=None):
        me = self.me
        far = 4 * (at + 1)

        @pl.when(self.plane > at)
        def _():
            owner = me - far
            self.arrived(part, owner)
            held = self.held(part, owner)

            @pl.when(self.plane < self.planes - 1)
            def _():
                self.copy(held, part, owner, self.up, me + 4).start()

            self.copy(held, part, owner, self.over, self.y_peer).start()
            if extra is not None:
                extra(part, owner)
            self.copy(held, part, owner, self.across, self.c_peer).start()

        @pl.when(self.plane + at + 1 < self.planes)
        def _():
            owner = me + far
            self.arrived(part, owner)
            held = self.held(part, owner)

            @pl.when(self.plane > 0)
            def _():
                self.copy(held, part, owner, self.down, me + self.count - 4).start()

            self.copy(held, part, owner, self.over, self.y_peer).start()
            if extra is not None:
                extra(part, owner)
            self.copy(held, part, owner, self.across, self.c_peer).start()

    def pass_across(self, part, owner, extra=None):
        self.arrived(part, owner)
        if extra is not None:
            extra(part, owner)
        self.copy(self.held(part, owner), part, owner, self.across, self.c_peer).start()

    def step_over(self, at, part, extra=None):
        if at < 0:
            self.pass_across(part, self.y_peer, extra)
            return
        far = 4 * (at + 1)

        @pl.when(self.plane > at)
        def _():
            self.pass_across(part, self.y_peer - far, extra)

        @pl.when(self.plane + at + 1 < self.planes)
        def _():
            self.pass_across(part, self.y_peer + far, extra)

    def column(self, base):
        return [(base + hop) % self.count for hop in range(0, self.count, 4)]

    def receive_across(self, part):
        both = self.c_peer + self.y_peer - self.me
        for owner in self.column(self.c_peer) + self.column(both):
            self.arrived(part, owner)

    def finish_sends(self, part):
        me = self.me
        for owner in self.column(me):
            plane = owner // 4

            @pl.when((plane <= self.plane) & (self.plane < self.planes - 1))
            def _():
                self.copy(self.held(part, owner), part, owner, self.up, me + 4).wait_send()

            @pl.when((plane >= self.plane) & (self.plane > 0))
            def _():
                place = me + self.count - 4
                self.copy(self.held(part, owner), part, owner, self.down, place).wait_send()

            self.copy(self.held(part, owner), part, owner, self.over, self.y_peer).wait_send()
        for owner in self.column(me) + self.column(self.y_peer):
            self.copy(self.held(part, owner), part, owner, self.across, self.c_peer).wait_send()


def relay_sems(parts, count):
    return [pltpu.SemaphoreType.DMA((parts, count)) for _ in range(5)]


def layer_kernel(
    count, scale, length_ref, stream_any, gain1_any, rows_any, out_any, gain2_any, pw1_any,
    taps_any, bn_gain_any, bn_bias_any, attended_ref, out_ref,
    stream_ref, gain1_ref, rows_ref, gain2_ref, taps_ref, gain_ref, bias_ref,
    x_ref, w_ref, xall, wcol, q_ref, k_ref, v_ref, parts_ref, wall, mixed_ref, landed,
    context, g_ref, low, high, padded, depth, mine, plane, near, far,
    f_up, f_down, f_over, f_across, f_landed, send_w, recv_w, twin_f,
    up, down, over, across, landed_w, twin_w, send_c, recv_c,
    halo_send, halo_recv, near_send, near_recv, far_send, far_recv, own_sem, get_sem,
):
    me = lax.axis_index("tm")
    call = lax.axis_index("call")
    twin = {"call": 1 - call, "tm": me}
    frames = Relay(count, xall, (f_up, f_down, f_over, f_across, f_landed))
    relay = Relay(count, wall, (up, down, over, across, landed_w))
    columns = parts_ref.shape[2]
    loads = (
        (stream_any, stream_ref),
        (gain1_any, gain1_ref),
        (rows_any, rows_ref),
        (out_any, parts_ref.at[0]),
        (pw1_any.at[:, pl.ds(0, columns)], parts_ref.at[1]),
        (pw1_any.at[:, pl.ds(columns, columns)], parts_ref.at[2]),
        (gain2_any, gain2_ref),
        (taps_any, taps_ref),
        (bn_gain_any, gain_ref),
        (bn_bias_any, bias_ref),
    )
    gets = [
        pltpu.make_async_copy(source, target, get_sem.at[at])
        for at, (source, target) in enumerate(loads)
    ]
    for get in gets:
        get.start()
    peers = []
    for flips in range(1, 8):
        spot, side = me, call
        if flips & 1:
            spot = spot + 1 - 2 * (me % 2)
        if flips & 2:
            spot = spot + 2 - 4 * ((me // 2) % 2)
        if flips & 4:
            side = 1 - call
        peers.append({"call": side, "tm": spot})
    hops = [{"tm": (me + hop) % count} for hop in range(4, count, 4)]
    barrier = pltpu.get_barrier_semaphore()
    places = [{"tm": (me + step) % count} for step in range(1, count)]
    places = places + [where for at, where in enumerate(peers) if at >= 3]
    for where in places:
        pl.semaphore_signal(barrier, inc=1, device_id=where, device_id_type=MESH)
    k_ref[0:LEFT, :] = jnp.zeros((LEFT, HEAD_DIM), jnp.bfloat16)
    v_ref[0:LEFT, :] = jnp.zeros((LEFT, HEAD_DIM), jnp.bfloat16)
    gets[0].wait()
    gets[1].wait()
    x_ref[...] = layer_norm(stream_ref[...], gain1_ref[...]).astype(jnp.bfloat16)
    own_x = pltpu.make_async_copy(x_ref, xall.at[0, me], own_sem.at[0])
    own_w = pltpu.make_async_copy(w_ref.at[me], wcol.at[me], own_sem.at[1])
    own_x.start()
    pl.semaphore_wait(barrier, len(places))
    frames.start(x_ref, 0)
    frames.start_across(x_ref, 0)
    for get in gets[2:]:
        get.wait()
    width = rows_ref.shape[1] // 3
    for head in range(count):
        for part in range(3):
            start = part * width + head * HEAD_DIM
            w_ref[head, :, part * HEAD_DIM : (part + 1) * HEAD_DIM] = rows_ref[
                :, start : start + HEAD_DIM
            ]
    own_w.start()

    def slice_to(place):
        return remote(
            w_ref.at[place], wcol.at[me], send_w.at[place], recv_w.at[me], {"tm": place}
        )

    def slice_on(owner):
        return remote(wcol.at[owner], wcol.at[owner], twin_f.at[owner], recv_w.at[owner], twin)

    @pl.when(me % 2 == call)
    def _():
        for step in range(1, count):
            slice_to((me + step) % count).start()

    steps = count // 4 - 1
    frames.step(0, 0)
    frames.step_over(-1, 0)
    for pair in range(count // 2):
        owner = 2 * pair + call

        @pl.when(owner != me)
        def _():
            slice_on(owner).wait_recv()
            slice_on(owner).start()

    for at in range(1, steps):
        frames.step(at, 0)
        frames.step_over(at - 1, 0)
    frames.step_over(steps - 1, 0)
    own = pltpu.make_async_copy(parts_ref, wall.at[:, me], own_sem.at[2])
    own.start()
    for part in (call, 2):
        relay.start(parts_ref.at[part], part)
    for part in range(3):
        relay.start_across(parts_ref.at[part], part)
    for pair in range(count // 2):
        owner, other = 2 * pair + call, 2 * pair + 1 - call

        @pl.when(other != me)
        def _():
            slice_on(other).wait_recv()

        @pl.when(owner != me)
        def _():
            slice_on(owner).wait_send()

    @pl.when(me % 2 == call)
    def _():
        for step in range(1, count):
            slice_to((me + step) % count).wait_send()

    own_x.wait()
    own_w.wait()
    frames.receive_across(0)
    w_columns = wcol[...].reshape(-1, 3 * HEAD_DIM)

    group = 4 * SPAN

    def project_group(at, carry):
        first = pl.multiple_of(at * group, group)
        rows = xall[0, pl.ds(4 * at, 4)].reshape(group, columns)
        packed = contract_with(rows, w_columns).astype(jnp.bfloat16)
        q_ref[pl.ds(first, group), :] = packed[:, :HEAD_DIM]
        k_ref[pl.ds(first + LEFT, group), :] = packed[:, HEAD_DIM : 2 * HEAD_DIM]
        v_ref[pl.ds(first + LEFT, group), :] = packed[:, 2 * HEAD_DIM :]
        return carry

    lax.fori_loop(0, count // 4, project_group, 0)

    def twin_copy(part, owner):
        return remote(
            wall.at[part, owner], wall.at[part, owner], twin_w.at[owner],
            landed_w.at[part, owner], twin,
        )

    def to_twin(part, owner):
        twin_copy(part, owner).start()

    width = LEFT + SPAN
    length = length_ref[call]

    def attend(block):
        first = pl.multiple_of(block * SPAN, SPAN)
        scores = lax.dot_general(
            q_ref[pl.ds(first, SPAN), :],
            k_ref[pl.ds(first, width), :],
            (((1,), (1,)), ((), ())),
            preferred_element_type=jnp.float32,
        )
        key_pos = block * SPAN - LEFT + lax.broadcasted_iota(jnp.int32, (SPAN, width), 1)
        query_pos = block * SPAN + lax.broadcasted_iota(jnp.int32, (SPAN, width), 0)
        allowed = (key_pos >= 0) & ((key_pos < length) | (key_pos == query_pos))
        raised = jnp.where(allowed, jnp.exp(scores * scale), 0.0)
        total = jnp.sum(raised, axis=-1, keepdims=True)
        shrink = jnp.where(total > 1.0, 2.0**-32, 1.0).astype(jnp.float32)
        probs = (raised * shrink * (1.0 / (total * shrink))).astype(jnp.bfloat16)
        mixed = jnp.dot(probs, v_ref[pl.ds(first, width), :], preferred_element_type=jnp.float32)
        return mixed.astype(jnp.bfloat16)

    def attend_and_send(step, carry):
        place = (me + step) % count
        mixed_ref[place] = attend(place)
        remote(
            mixed_ref.at[place], landed.at[me], send_c.at[place], recv_c.at[me], {"tm": place}
        ).start()
        return carry

    def relay_step(at):
        relay.step(at, call, to_twin)
        relay.step(at, 2)
        relay.step_over(at - 1, call, to_twin)
        relay.step_over(at - 1, 2)

    lax.fori_loop(1, count // 2, attend_and_send, 0)
    relay_step(0)
    lax.fori_loop(count // 2, count, attend_and_send, 0)
    landed[me] = attend(me)
    for at in range(1, steps):
        relay_step(at)
    relay.step_over(steps - 1, call, to_twin)
    relay.step_over(steps - 1, 2)
    received = relay.column(me)[1:] + relay.column(relay.y_peer)
    for owner in received:
        relay.pass_across(1 - call, owner)
    for step in range(1, count):
        owner = (me + step) % count
        remote(
            mixed_ref.at[owner], landed.at[owner], send_c.at[owner], recv_c.at[owner],
            {"tm": owner},
        ).wait()
    for pair in range(0, count, 2):
        context[:, pair * HEAD_DIM : (pair + 2) * HEAD_DIM] = jnp.concatenate(
            [landed[pair], landed[pair + 1]], axis=1
        )
    own.wait()
    for part in range(3):
        relay.receive_across(part)
    rows, width = depth.shape
    valid = me * rows + lax.broadcasted_iota(jnp.int32, (rows, 1), 0) < length
    weights = [wall[part].reshape(width, width) for part in range(3)]
    wide = stream_ref[...].astype(jnp.float32) + contract_with(context[...], weights[0])
    attended = jnp.where(valid, wide, 0.0).astype(jnp.bfloat16)
    attended_ref[...] = attended
    conv_in = layer_norm(attended, gain2_ref[...]).astype(jnp.bfloat16)
    gate = jax.nn.sigmoid(contract_with(conv_in, weights[2]))
    gated = contract_with(conv_in, weights[1]) * gate
    g_ref[...] = jnp.where(valid, gated, 0.0).astype(jnp.bfloat16)
    right, left = (me + 1) % count, (me + count - 1) % count
    to_right = remote(
        g_ref.at[pl.ds(rows - EDGE, EDGE)], low, halo_send.at[0], halo_recv.at[0], {"tm": right}
    )
    to_left = remote(
        g_ref.at[pl.ds(0, EDGE)], high, halo_send.at[1], halo_recv.at[1], {"tm": left}
    )
    to_right.start()
    to_left.start()
    padded[EDGE : EDGE + rows, :] = g_ref[...].astype(jnp.float32)
    to_right.wait_recv()
    to_left.wait_recv()
    has_low = jnp.where(me > 0, 1.0, 0.0).astype(jnp.float32)
    has_high = jnp.where(me < count - 1, 1.0, 0.0).astype(jnp.float32)
    padded[0:EDGE, :] = low[...].astype(jnp.float32) * has_low
    padded[EDGE + rows : 2 * EDGE + rows, :] = high[...].astype(jnp.float32) * has_high
    first = me * rows + lax.broadcasted_iota(jnp.int32, (rows, 1), 0)
    valid = jnp.where(first < length_ref[call], 1.0, 0.0).astype(jnp.float32)
    for at in range(0, width, STRIP):
        strip = slice(at, at + STRIP)
        total = jnp.zeros((rows, STRIP), jnp.float32)
        for tap in range(KERNEL):
            start = EDGE - KERNEL // 2 + tap
            total = total + padded[start : start + rows, strip] * taps_ref[tap : tap + 1, strip]
        depth[:, strip] = total
        masked = total * valid
        mine[0:1, strip] = jnp.sum(masked, axis=0, keepdims=True)
        mine[1:2, strip] = jnp.sum(masked * total, axis=0, keepdims=True)
    near_copies = []
    for slot, where in enumerate(peers):
        copy = remote(mine, near.at[slot], near_send.at[slot], near_recv.at[slot], where)
        copy.start()
        near_copies.append(copy)
    for copy in near_copies:
        copy.wait_recv()
    both = mine[...]
    for slot in range(len(peers)):
        both = both + near[slot]
    plane[...] = both
    far_copies = []
    for slot, where in enumerate(hops):
        copy = remote(plane, far.at[slot], far_send.at[slot], far_recv.at[slot], where)
        copy.start()
        far_copies.append(copy)
    for copy in far_copies:
        copy.wait_recv()
    for slot in range(len(hops)):
        both = both + far[slot]
    both = both / (length_ref[0] + length_ref[1]).astype(jnp.float32)
    average = both[0:1]
    spread = lax.rsqrt(both[1:2] - average * average + 1e-05)
    for at in range(0, width, STRIP):
        strip = slice(at, at + STRIP)
        act = (depth[:, strip] - average[:, strip]) * spread[:, strip]
        act = act * gain_ref[:, strip] + bias_ref[:, strip]
        act = act * jax.nn.sigmoid(act)
        out_ref[:, strip] = jnp.where(valid > 0.0, act, 0.0).astype(out_ref.dtype)
    for copy in [to_right, to_left] + near_copies + far_copies:
        copy.wait_send()


    for owner in received:
        twin_copy(call, owner).wait_send()
    relay.finish_sends(call)
    relay.finish_sends(2)
    for owner in relay.column(me) + relay.column(relay.y_peer):
        relay.copy(wall.at[1 - call, owner], 1 - call, owner, across, relay.c_peer).wait_send()
    frames.finish_sends(0)


def layer_call(lengths, stream, gain1, w_qkv, w_out, gain2, w_pw1, taps, bn_gain, bn_bias):
    rows, width = stream.shape
    count = lax.axis_size("tm")
    wide, deep = jnp.float32, jnp.bfloat16
    depth, planes = w_out.shape[0], count // 4
    total = count * rows
    anywhere = pl.BlockSpec(memory_space=pl.ANY)
    vmem = pl.BlockSpec(memory_space=pltpu.VMEM)
    buffers = [
        (stream.shape, deep), ((1, width), wide), (w_qkv.shape, deep), ((1, width), wide),
        (taps.shape, wide), ((1, width), wide), ((1, width), wide),
        (stream.shape, deep), ((count, depth, 3 * HEAD_DIM), deep),
        ((1, count, rows, width), deep), ((count, depth, 3 * HEAD_DIM), deep),
        ((total, HEAD_DIM), deep), ((total + LEFT, HEAD_DIM), deep),
        ((total + LEFT, HEAD_DIM), deep),
        ((3, depth, width), deep), ((3, count, depth, width), deep),
        ((count, rows, HEAD_DIM), deep), ((count, rows, HEAD_DIM), deep),
        (stream.shape, deep), (stream.shape, deep), ((EDGE, width), deep), ((EDGE, width), deep),
        ((rows + 2 * EDGE, width), wide), ((rows, width), wide), ((2, width), wide),
        ((2, width), wide), ((7, 2, width), wide), ((planes - 1, 2, width), wide),
    ]
    counts = [(count,)] * 3, [(count,)] * 3, [2, 2, 7, 7, planes - 1, planes - 1, 3, 10]
    sems = pltpu.SemaphoreType.DMA
    return pl.pallas_call(
        functools.partial(layer_kernel, count, HEAD_DIM**-0.5),
        out_shape=(jax.ShapeDtypeStruct(stream.shape, deep),) * 2,
        in_specs=[pl.BlockSpec(memory_space=pltpu.SMEM)] + [anywhere] * 9,
        out_specs=(vmem, vmem),
        scratch_shapes=[pltpu.VMEM(shape, kind) for shape, kind in buffers]
        + relay_sems(1, count)
        + [sems(shape) for shape in counts[0]]
        + relay_sems(3, count)
        + [sems(shape) for shape in counts[1]]
        + [sems((size,)) for size in counts[2]],
        compiler_params=pltpu.CompilerParams(
            collective_id=0, has_side_effects=True, vmem_limit_bytes=48 * 1024 * 1024
        ),
        name="layer",
    )(lengths, stream, gain1, w_qkv, w_out, gain2, w_pw1, taps, bn_gain, bn_bias)


def one_head_each(
    frames, lengths, ln_attn_gain, w_qkv, w_out, ln_conv_gain, w_pw1, dw_kernel, bn_gain, bn_bias
):
    attended, conv_act = layer_call(
        lengths, frames[0], ln_attn_gain[None], w_qkv, w_out, ln_conv_gain[None], w_pw1,
        dw_kernel, bn_gain[None], bn_bias[None],
    )
    return (attended[None], conv_act[None])


def fits_one_head(mesh):
    return mesh.shape["tm"] == 16 and mesh.shape["call"] == 2


def solution(mesh):
    return jax.shard_map(
        one_head_each if fits_one_head(mesh) else on_device,
        mesh=mesh,
        in_specs=(
            P("call", "tm", None),
            P(),
            P(),
            P("tm", None),
            P("tm", None),
            P(),
            P("tm", None),
            P(),
            P(),
            P(),
        ),
        out_specs=(P("call", "tm", None), P("call", "tm", None)),
        check_vma=False,
    )
```
